32 devices in a mesh: segment: 8 (over z, core), node: 4 (over y, x).
Axes of the slice: x: 2, y: 2, z: 4, core: 2. Of those that a mesh axis runs over, the one named last changes fastest.
Arguments:
- features: bfloat16 [2, 2048, 256], P(None, 'node'), may hold values from -6 to 6
- tiles: bfloat16 [2, 16, 8, 128, 128], P(None, 'node'), may hold values from -0.25 to 0.25
- tile_cols: int32 [2, 16, 8], P(None, 'node'), may hold values from 0 to 15, as said below
- tile_count: int32 [2, 16], P(None, 'node'), may hold values from 1 to 8
- weights: bfloat16 [8, 256, 256], P('segment'), may hold values from -0.375 to 0.375
Outputs:
- layer_outputs: bfloat16 [8, 2, 2048, 256], P('segment', None, 'node')
The draws below stay inside these ranges and needn't reach their ends.
Inputs may be any that keep to these rules, and one draw needn't show every extreme that they name: `tile_cols`: with P = 4 block rows per node group of 512 nodes, the block column of a tile in block row b lies in group g - 1, g or g + 1 (counted modulo 2048 / 512 groups) where g = b // P is the group of b. `tile_count`: slots from the count on are padding.
All inputs are finite; a program needn't handle non-finite values.
Results may differ from the reference program's by a relative error of at most 0.011.
Values may be sent and summed in bfloat16 or wider, within the bound.
A program may use at most 64 MiB of HBM per device.

```python
import jax
import jax.numpy as jnp
from jax import lax

D = 256
TILE = 128
SLOTS = 8
SPANS = 2
ROWS_DEV = 512
LAYERS = 8
SPAN = 2048
NB = 16
N_NODE = 4


def draw_tile_cols(key, part):
    per_group = ROWS_DEV // TILE
    key_side, key_inner = jax.random.split(jax.random.fold_in(key, 17))
    side = jax.random.randint(key_side, (SPANS, NB, SLOTS), -1, 2, dtype=jnp.int32)
    inner = jax.random.randint(key_inner, (SPANS, NB, SLOTS), 0, per_group, dtype=jnp.int32)
    owner = jnp.arange(NB, dtype=jnp.int32) // per_group
    group = (owner[None, :, None] + side + N_NODE) % N_NODE
    return (group * per_group + inner).astype(jnp.int32)


def plant(result, rng, low, high):
    spot = [jax.random.randint(jax.random.fold_in(rng, axis), (), 0, length) for axis, length in enumerate(result.shape)]
    longest = result.shape.index(max(result.shape))
    beside = spot[:longest] + [(spot[longest] + 1) % result.shape[longest]] + spot[longest + 1:]
    return result.at[tuple(spot)].set(low).at[tuple(beside)].set(high)


def level_of(key, extent, pieces, smallest, top_value):
    def one(dim, blocks):
        draws = jax.random.uniform(jax.random.fold_in(jax.random.fold_in(key, 6), dim), (blocks,), jnp.float32, smallest / len(pieces), top_value / len(pieces))
        return jnp.repeat(jnp.exp(draws), extent[dim] // blocks).reshape((-1,) + (1,) * (len(extent) - dim - 1))

    loudness = one(*pieces[0])
    for cut in pieces[1:]:
        loudness = loudness * one(*cut)
    return loudness


def bell_draw(own_key, dims, deviation, most, cuts=(), kind=jnp.bfloat16):
    result = deviation * jax.random.normal(own_key, dims, jnp.float32)
    if cuts:
        result = result * level_of(own_key, dims, cuts, -0.22, 0.18)
    return jnp.clip(result, -most, most).astype(kind)


def setup_inputs(seed: int = 0) -> dict:
    splits = jax.random.split(jax.random.key(seed), 6)
    return {
        "features": bell_draw(splits[0], (SPANS, SPAN, D), 1.0, 6.0, ((1, 4),)),
        "tiles": bell_draw(splits[1], (SPANS, NB, SLOTS, TILE, TILE), (4 * TILE) ** -0.5, 0.25, ((1, 4),)),
        "tile_cols": draw_tile_cols(jax.random.fold_in(splits[5], 71), 0),
        "tile_count": plant(jax.random.randint(splits[3], (SPANS, NB), 1, SLOTS + 1), jax.random.fold_in(splits[3], 1), 1, SLOTS).astype(jnp.int32),
        "weights": bell_draw(splits[4], (LAYERS, D, D), D ** -0.5, 0.375, ((0, 8),)),
    }


def layer_rows(hidden, masked, columns, initial, weight, beta_mix):
    grouped = hidden.reshape(NB, TILE, D)
    picked = grouped[columns]
    aggregate = jnp.einsum("bkij,bkjd->bid", masked.astype(jnp.float32), picked.astype(jnp.float32)).reshape(SPAN, D)
    support = (0.9 * aggregate + 0.1 * initial.astype(jnp.float32)).astype(jnp.bfloat16)
    branch = jnp.dot(support, weight, preferred_element_type=jnp.float32)
    combined = (1.0 - beta_mix) * support.astype(jnp.float32) + beta_mix * branch
    return jnp.maximum(combined, 0.0).astype(jnp.bfloat16)


def reference(features, tiles, tile_cols, tile_count, weights):
    slot_ids = jnp.arange(SLOTS, dtype=jnp.int32)
    live = (slot_ids[None, None, :] < tile_count[:, :, None]).astype(jnp.bfloat16)
    masked = tiles * live[:, :, :, None, None]
    layer_ids = jnp.arange(LAYERS, dtype=jnp.float32)
    betas = jnp.log(0.5 / (layer_ids + 1.0) + 1.0)

    def one_layer(hidden, inputs):
        weight, beta_mix = inputs
        results = jnp.stack([layer_rows(hidden[k], masked[k], tile_cols[k], features[k], weight, beta_mix) for k in range(SPANS)])
        return results, results

    final, stacked = lax.scan(one_layer, features, (weights, betas))
    return stacked
```

```python
import jax
import jax.numpy as jnp
import numpy as np
from jax import lax
from jax.experimental import pallas as pl
from jax.experimental.pallas import tpu as pltpu
from jax.sharding import PartitionSpec as P


def with_halo(array, sides, width):
    for axis, dim in sides:
        count, length = (lax.axis_size(axis), array.shape[dim])
        up = [(i, (i + 1) % count) for i in range(count)]
        down = [(j, i) for i, j in up]
        last = lax.slice_in_dim(array, length - width, length, axis=dim)
        first = lax.slice_in_dim(array, 0, width, axis=dim)
        before = lax.ppermute(last, axis, up)
        after = lax.ppermute(first, axis, down)
        array = jnp.concatenate([before, array, after], axis=dim)
    return array


def passed_along(block, axis, distance):
    devices = range(lax.axis_size(axis))
    route = [(i - distance, i) for i in devices if i - distance in devices]
    return lax.ppermute(block, axis, route)


def layer_rows(window, masked, columns, initial, weight, beta_mix):
    tile_size = masked.shape[-1]
    feature_width = window.shape[-1]
    grouped = window.reshape(window.shape[0] // tile_size, tile_size, feature_width)
    picked = grouped[columns]
    aggregate = jnp.einsum("bkij,bkjd->bid", masked, picked, preferred_element_type=jnp.float32)
    aggregate = aggregate.reshape(-1, feature_width)
    support = (0.9 * aggregate + 0.1 * initial.astype(jnp.float32)).astype(jnp.bfloat16)
    branch = jnp.dot(support, weight, preferred_element_type=jnp.float32)
    combined = (1.0 - beta_mix) * support.astype(jnp.float32) + beta_mix * branch
    return jnp.maximum(combined, 0.0).astype(jnp.bfloat16)


def on_device(features, tiles, tile_cols, tile_count, weights):
    segments = lax.axis_size("segment")
    groups = lax.axis_size("node")
    segment_id = lax.axis_index("segment")
    group_id = lax.axis_index("node")
    spans = features.shape[0]
    per_group = tiles.shape[1]
    total_blocks = per_group * groups
    first_block = (group_id - 1) * per_group
    local_cols = (tile_cols - first_block + total_blocks) % total_blocks
    slot_ids = jnp.arange(tiles.shape[2], dtype=jnp.int32)
    live = (slot_ids[None, None, :] < tile_count[:, :, None]).astype(jnp.bfloat16)
    masked = tiles * live[:, :, :, None, None]
    beta_mix = jnp.log(0.5 / (segment_id.astype(jnp.float32) + 1.0) + 1.0)
    weight = weights[0]
    rows_here = features.shape[1]

    def step(step_no, state_pair):
        incoming, stored = state_pair
        offset_now = step_no - segment_id
        active = (offset_now >= 0) & (offset_now < spans)
        span_id = jnp.clip(offset_now, 0, spans - 1)
        initial = lax.dynamic_index_in_dim(features, span_id, 0, keepdims=False)
        layer_input = jnp.where(segment_id == 0, initial, incoming)
        window = with_halo(layer_input, (("node", 0),), rows_here)
        span_tiles = lax.dynamic_index_in_dim(masked, span_id, 0, keepdims=False)
        span_cols = lax.dynamic_index_in_dim(local_cols, span_id, 0, keepdims=False)
        result = layer_rows(window, span_tiles, span_cols, initial, weight, beta_mix)
        updated = lax.dynamic_update_index_in_dim(stored, result, span_id, 0)
        stored = jnp.where(active, updated, stored)
        incoming = passed_along(result, "segment", 1)
        return (incoming, stored)

    start_pair = (
        jnp.zeros(features.shape[1:], jnp.bfloat16),
        jnp.zeros(features.shape, jnp.bfloat16),
    )
    final_pair = lax.fori_loop(0, segments + spans - 1, step, start_pair)
    stored = final_pair[1]
    return stored[None]


MESH = pl.DeviceIdType.MESH


def gather_kernel(tiles, feats, cols, counts, weight, a_all, f_all, c_all, n_all, w_all,
                  loc_sem, ls, lr, cs, cr, ms, mr, ws, wr, ks, kr):
    seg = lax.axis_index("segment")
    g = lax.axis_index("node")
    c = seg % 2
    z = seg // 2
    span = z % 2
    xn = g + 1 - 2 * (g % 2)
    yn = (g + 2) % 4
    dn = 3 - g
    peer = seg + 1 - 2 * c
    others = [((z + d) % 4) * 2 + c for d in range(1, 4)]

    barrier = pltpu.get_barrier_semaphore()
    for n in (xn, yn, dn):
        pl.semaphore_signal(barrier, inc=1, device_id={"node": n}, device_id_type=MESH)
    for s in [peer] + others:
        pl.semaphore_signal(barrier, inc=1, device_id={"segment": s}, device_id_type=MESH)
    pl.semaphore_wait(barrier, 7)

    half = pl.ds(c * 2, 2)

    def piece(group, part):
        row = c * 2 + part
        return (a_all.at[group, row], f_all.at[group, pl.ds(row * 128, 128)])

    def send(src, dst, ssem, rsem, dev):
        out = []
        for k in range(2):
            cp = pltpu.make_async_remote_copy(src[k], dst[k], ssem.at[k], rsem.at[k],
                                              device_id=dev, device_id_type=MESH)
            cp.start()
            out.append(cp)
        return out

    def own(part):
        row = c * 2 + part
        return (tiles.at[span, row], feats.at[span, pl.ds(row * 128, 128)])

    xa = send(own(0), piece(g, 0), ls.at[0], lr.at[0], {"node": xn})
    yb = send(own(1), piece(g, 1), ls.at[3], lr.at[3], {"node": yn})
    xb = send(own(1), piece(g, 1), ls.at[1], lr.at[1], {"node": xn})
    ya = send(own(0), piece(g, 0), ls.at[2], lr.at[2], {"node": yn})
    wcopies = []
    for d in range(3):
        cp = pltpu.make_async_remote_copy(weight.at[0], w_all.at[seg], ws.at[d], wr.at[d],
                                          device_id={"segment": others[d]}, device_id_type=MESH)
        cp.start()
        wcopies.append(cp)
    kcopies = [pltpu.make_async_remote_copy(weight.at[0], w_all.at[seg], ks.at[3], kr.at[3],
                                            device_id={"segment": peer}, device_id_type=MESH)]
    kcopies[0].start()
    mcopies = []
    for d, n in enumerate((xn, yn, dn)):
        for k, (s, t) in enumerate(((cols, c_all), (counts, n_all))):
            cp = pltpu.make_async_remote_copy(s, t.at[g], ms.at[d, k], mr.at[d, k],
                                              device_id={"node": n}, device_id_type=MESH)
            cp.start()
            mcopies.append(cp)
    local = []
    for k, (s, t) in enumerate(((tiles.at[span], a_all.at[g]), (feats.at[span], f_all.at[g]),
                                (cols, c_all.at[g]), (counts, n_all.at[g]), (weight.at[0], w_all.at[seg]))):
        cp = pltpu.make_async_copy(s, t, loc_sem.at[k])
        cp.start()
        local.append(cp)

    def arrived(copies):
        for cp in copies:
            cp.wait_recv()

    core = []

    def share(group, part, idx):
        p = piece(group, part)
        core.append(send(p, p, cs.at[idx], cr.at[idx], {"segment": peer}))

    arrived(xa)
    p = piece(xn, 0)
    da = send(p, p, ls.at[4], lr.at[4], {"node": yn})
    share(xn, 0, 0)
    arrived(yb)
    p = piece(yn, 1)
    db = send(p, p, ls.at[5], lr.at[5], {"node": xn})
    share(yn, 1, 3)
    for d in range(3):
        wcopies[d].wait_recv()
        src = ((z + 3 - d) % 4) * 2 + c
        cp = pltpu.make_async_remote_copy(w_all.at[src], w_all.at[src], ks.at[d], kr.at[d],
                                          device_id={"segment": peer}, device_id_type=MESH)
        cp.start()
        kcopies.append(cp)
    arrived(xb)
    share(xn, 1, 1)
    arrived(ya)
    share(yn, 0, 2)
    arrived(da)
    share(dn, 0, 4)
    arrived(db)
    share(dn, 1, 5)
    for cp in mcopies:
        cp.wait()
    for group in (xa, xb, ya, yb, da, db):
        for cp in group:
            cp.wait_send()
    for cp in wcopies:
        cp.wait_send()
    for cp in kcopies:
        cp.wait()
    for group in core:
        for cp in group:
            cp.wait()
    for cp in local:
        cp.wait()


def compute_kernel(cols, counts, betas, a_all, f_all, w_all, own_out, other_out, dense, acc, hid):
    seg = lax.axis_index("segment")
    me = lax.axis_index("node")
    c = seg % 2
    z = seg // 2
    span = z % 2
    partner = (z + 1 - 2 * span) * 2 + c
    last = jnp.maximum(seg, partner)
    rows = 512

    def densify(b, carry):
        grp = b // 4
        row = b % 4
        acc[...] = jnp.zeros_like(acc)

        def slot(k, carry):
            j = (cols[grp, span, row, k] - 4 * (grp - 1) + 16) % 16
            acc[j] += a_all[grp, row, k].astype(jnp.float32)
            return carry

        lax.fori_loop(0, counts[grp, span, row], slot, 0)
        for j in range(12):
            dense[b, :, j * 128:(j + 1) * 128] = acc[j].astype(jnp.bfloat16)
        return carry

    lax.fori_loop(0, 16, densify, 0)

    def put(buf, grp, value):
        hid[buf, (grp + 1) * rows:(grp + 2) * rows, :] = value
        if grp == 3:
            hid[buf, 0:rows, :] = value
        if grp == 0:
            hid[buf, 5 * rows:6 * rows, :] = value

    for grp in range(4):
        put(0, grp, f_all[grp])

    def layer(l, carry):
        cur = l % 2
        nxt = 1 - cur
        beta = betas[l]
        for grp in range(4):
            rel = (grp - me + 4) % 4
            dist = jnp.minimum(rel, 4 - rel)

            @pl.when(dist <= last - l)
            def _():
                lhs = dense[grp * 4:(grp + 1) * 4].reshape(rows, 12 * 128)
                agg = jnp.dot(lhs, hid[cur, grp * rows:(grp + 3) * rows, :],
                              preferred_element_type=jnp.float32)
                sup = (0.9 * agg + 0.1 * f_all[grp].astype(jnp.float32)).astype(jnp.bfloat16)
                branch = jnp.dot(sup, w_all[l], preferred_element_type=jnp.float32)
                res = (1.0 - beta) * sup.astype(jnp.float32) + beta * branch
                put(nxt, grp, jnp.maximum(res, 0.0).astype(jnp.bfloat16))

        mine = pl.ds(pl.multiple_of((me + 1) * rows, rows), rows)

        @pl.when(l == seg)
        def _():
            own_out[...] = hid[nxt, mine, :]

        @pl.when(l == partner)
        def _():
            other_out[...] = hid[nxt, mine, :]

        return carry

    lax.fori_loop(0, last + 1, layer, 0)


def whole_spans(features, tiles, tile_cols, tile_count, weights):
    seg = lax.axis_index("segment")
    span = (seg // 2) % 2
    any_spec = pl.BlockSpec(memory_space=pl.ANY)
    bf = jnp.bfloat16
    dma = pltpu.SemaphoreType.DMA
    a_all, f_all, c_all, n_all, w_all = pl.pallas_call(
        gather_kernel,
        out_shape=[
            jax.ShapeDtypeStruct((4,) + tiles.shape[1:], bf),
            jax.ShapeDtypeStruct((4,) + features.shape[1:], bf),
            jax.ShapeDtypeStruct((4,) + tile_cols.shape, jnp.int32),
            jax.ShapeDtypeStruct((4,) + tile_count.shape, jnp.int32),
            jax.ShapeDtypeStruct((8,) + weights.shape[1:], bf),
        ],
        in_specs=[any_spec] * 5,
        out_specs=[any_spec] * 5,
        scratch_shapes=[dma((5,)), dma((6, 2)), dma((6, 2)), dma((6, 2)), dma((6, 2)),
                        dma((3, 2)), dma((3, 2)), dma((3,)), dma((3,)), dma((4,)), dma((4,))],
        compiler_params=pltpu.CompilerParams(collective_id=0, has_side_effects=True),
        name="gather",
    )(tiles, features, tile_cols, tile_count, weights)
    betas = jnp.asarray(np.log(0.5 / (np.arange(8, dtype=np.float32) + 1.0) + 1.0), jnp.float32)
    smem = pl.BlockSpec(memory_space=pltpu.SMEM)
    vmem = pl.BlockSpec(memory_space=pltpu.VMEM)
    row_shape = jax.ShapeDtypeStruct(features.shape[1:], bf)
    own, other = pl.pallas_call(
        compute_kernel,
        out_shape=[row_shape, row_shape],
        in_specs=[smem, smem, smem, vmem, vmem, vmem],
        out_specs=[vmem, vmem],
        scratch_shapes=[pltpu.VMEM((16, 128, 1536), bf), pltpu.VMEM((12, 128, 128), jnp.float32),
                        pltpu.VMEM((2, 3072, 256), bf)],
        compiler_params=pltpu.CompilerParams(vmem_limit_bytes=48 * 1024 * 1024),
        name="layers",
    )(c_all, n_all, betas, a_all, f_all, w_all)
    other = lax.ppermute(other, "segment", [(s, s ^ 2) for s in range(8)])
    first = jnp.where(span == 0, own, other)
    second = jnp.where(span == 0, other, own)
    return jnp.stack([first, second])[None]


def solution(mesh):
    in_specs = (
        P(None, "node", None),
        P(None, "node", None, None, None),
        P(None, "node", None),
        P(None, "node"),
        P("segment", None, None),
    )
    out_specs = P("segment", None, "node", None)
    small = mesh.shape["segment"] == 8 and mesh.shape["node"] == 4
    return jax.shard_map(
        whole_spans if small else on_device, mesh=mesh, in_specs=in_specs, out_specs=out_specs, check_vma=False
    )
```

```python
import jax
import jax.numpy as jnp
import numpy as np
from jax import lax
from jax.experimental import pallas as pl
from jax.experimental.pallas import tpu as pltpu
from jax.sharding import PartitionSpec as P


def with_halo(array, sides, width):
    for axis, dim in sides:
        count, length = (lax.axis_size(axis), array.shape[dim])
        up = [(i, (i + 1) % count) for i in range(count)]
        down = [(j, i) for i, j in up]
        last = lax.slice_in_dim(array, length - width, length, axis=dim)
        first = lax.slice_in_dim(array, 0, width, axis=dim)
        before = lax.ppermute(last, axis, up)
        after = lax.ppermute(first, axis, down)
        array = jnp.concatenate([before, array, after], axis=dim)
    return array


def passed_along(block, axis, distance):
    devices = range(lax.axis_size(axis))
    route = [(i - distance, i) for i in devices if i - distance in devices]
    return lax.ppermute(block, axis, route)


def layer_rows(window, masked, columns, initial, weight, beta_mix):
    tile_size = masked.shape[-1]
    feature_width = window.shape[-1]
    grouped = window.reshape(window.shape[0] // tile_size, tile_size, feature_width)
    picked = grouped[columns]
    aggregate = jnp.einsum("bkij,bkjd->bid", masked, picked, preferred_element_type=jnp.float32)
    aggregate = aggregate.reshape(-1, feature_width)
    support = (0.9 * aggregate + 0.1 * initial.astype(jnp.float32)).astype(jnp.bfloat16)
    branch = jnp.dot(support, weight, preferred_element_type=jnp.float32)
    combined = (1.0 - beta_mix) * support.astype(jnp.float32) + beta_mix * branch
    return jnp.maximum(combined, 0.0).astype(jnp.bfloat16)


def on_device(features, tiles, tile_cols, tile_count, weights):
    segments = lax.axis_size("segment")
    groups = lax.axis_size("node")
    segment_id = lax.axis_index("segment")
    group_id = lax.axis_index("node")
    spans = features.shape[0]
    per_group = tiles.shape[1]
    total_blocks = per_group * groups
    first_block = (group_id - 1) * per_group
    local_cols = (tile_cols - first_block + total_blocks) % total_blocks
    slot_ids = jnp.arange(tiles.shape[2], dtype=jnp.int32)
    live = (slot_ids[None, None, :] < tile_count[:, :, None]).astype(jnp.bfloat16)
    masked = tiles * live[:, :, :, None, None]
    beta_mix = jnp.log(0.5 / (segment_id.astype(jnp.float32) + 1.0) + 1.0)
    weight = weights[0]
    rows_here = features.shape[1]

    def step(step_no, state_pair):
        incoming, stored = state_pair
        offset_now = step_no - segment_id
        active = (offset_now >= 0) & (offset_now < spans)
        span_id = jnp.clip(offset_now, 0, spans - 1)
        initial = lax.dynamic_index_in_dim(features, span_id, 0, keepdims=False)
        layer_input = jnp.where(segment_id == 0, initial, incoming)
        window = with_halo(layer_input, (("node", 0),), rows_here)
        span_tiles = lax.dynamic_index_in_dim(masked, span_id, 0, keepdims=False)
        span_cols = lax.dynamic_index_in_dim(local_cols, span_id, 0, keepdims=False)
        result = layer_rows(window, span_tiles, span_cols, initial, weight, beta_mix)
        updated = lax.dynamic_update_index_in_dim(stored, result, span_id, 0)
        stored = jnp.where(active, updated, stored)
        incoming = passed_along(result, "segment", 1)
        return (incoming, stored)

    start_pair = (
        jnp.zeros(features.shape[1:], jnp.bfloat16),
        jnp.zeros(features.shape, jnp.bfloat16),
    )
    final_pair = lax.fori_loop(0, segments + spans - 1, step, start_pair)
    stored = final_pair[1]
    return stored[None]


MESH = pl.DeviceIdType.MESH


def gather_kernel(tiles, feats, cols, counts, weight, a_all, f_all, c_all, n_all, w_all,
                  loc_sem, ls, lr, cs, cr, ms, mr, ws, wr, ks, kr):
    seg = lax.axis_index("segment")
    g = lax.axis_index("node")
    c = seg % 2
    z = seg // 2
    span = z % 2
    xn = g + 1 - 2 * (g % 2)
    yn = (g + 2) % 4
    dn = 3 - g
    peer = seg + 1 - 2 * c
    others = [((z + d) % 4) * 2 + c for d in range(1, 4)]

    barrier = pltpu.get_barrier_semaphore()
    for n in (xn, yn, dn):
        pl.semaphore_signal(barrier, inc=1, device_id={"node": n}, device_id_type=MESH)
    for s in [peer] + others:
        pl.semaphore_signal(barrier, inc=1, device_id={"segment": s}, device_id_type=MESH)
    pl.semaphore_wait(barrier, 7)

    ln = xn * (1 - c) + yn * c
    on = yn * (1 - c) + xn * c

    def mine(i):
        return (i + 2 * c) % 4

    def theirs(i):
        return (i + 2 - 2 * c) % 4

    def piece(group, row):
        return (a_all.at[group, row], f_all.at[group, pl.ds(row * 128, 128)])

    def send(src, dst, ssem, rsem, dev):
        out = []
        for k in range(2):
            cp = pltpu.make_async_remote_copy(src[k], dst[k], ssem.at[k], rsem.at[k],
                                              device_id=dev, device_id_type=MESH)
            cp.start()
            out.append(cp)
        return out

    link = []
    for i in range(4):
        row = mine(i)
        link.append(send((tiles.at[span, row], feats.at[span, pl.ds(row * 128, 128)]),
                         piece(g, row), ls.at[i], lr.at[i], {"node": ln}))
    wcopies = []
    for d in range(3):
        cp = pltpu.make_async_remote_copy(weight.at[0], w_all.at[seg], ws.at[d], wr.at[d],
                                          device_id={"segment": others[d]}, device_id_type=MESH)
        cp.start()
        wcopies.append(cp)
    kcopies = [pltpu.make_async_remote_copy(weight.at[0], w_all.at[seg], ks.at[3], kr.at[3],
                                            device_id={"segment": peer}, device_id_type=MESH)]
    kcopies[0].start()
    mcopies = []
    for d, n in enumerate((xn, yn, dn)):
        for k, (s, t) in enumerate(((cols, c_all), (counts, n_all))):
            cp = pltpu.make_async_remote_copy(s, t.at[g], ms.at[d, k], mr.at[d, k],
                                              device_id={"node": n}, device_id_type=MESH)
            cp.start()
            mcopies.append(cp)
    local = []
    for k, (s, t) in enumerate(((tiles.at[span], a_all.at[g]), (feats.at[span], f_all.at[g]),
                                (cols, c_all.at[g]), (counts, n_all.at[g]), (weight.at[0], w_all.at[seg]))):
        cp = pltpu.make_async_copy(s, t, loc_sem.at[k])
        cp.start()
        local.append(cp)

    def arrived(copies):
        for cp in copies:
            cp.wait_recv()

    core = {}

    def share(group, row, idx):
        p = piece(group, row)
        core[idx] = send(p, p, cs.at[idx], cr.at[idx], {"segment": peer})

    def forward(i):
        p = piece(on, theirs(i))
        link.append(send(p, p, ls.at[4 + i], lr.at[4 + i], {"node": ln}))

    for i in range(2):
        arrived(link[i])
        share(ln, mine(i), i)
    for i in range(2):
        arrived(core[i])
        forward(i)
    for i in range(2, 4):
        arrived(link[i])
        share(ln, mine(i), i)
    for d in range(3):
        wcopies[d].wait_recv()
        src = ((z + 3 - d) % 4) * 2 + c
        cp = pltpu.make_async_remote_copy(w_all.at[src], w_all.at[src], ks.at[d], kr.at[d],
                                          device_id={"segment": peer}, device_id_type=MESH)
        cp.start()
        kcopies.append(cp)
    for i in range(2):
        arrived(link[4 + i])
        share(dn, theirs(i), 4 + i)
    for i in range(2, 6):
        arrived(core[i])
    for cp in mcopies + kcopies:
        cp.wait()
    for group in link + list(core.values()):
        for cp in group:
            cp.wait_send()
    for cp in wcopies:
        cp.wait_send()
    for cp in local:
        cp.wait()


def compute_kernel(cols, counts, betas, a_all, f_all, w_all, own_out, other_out, dense, acc, hid):
    seg = lax.axis_index("segment")
    me = lax.axis_index("node")
    c = seg % 2
    z = seg // 2
    span = z % 2
    partner = (z + 1 - 2 * span) * 2 + c
    last = jnp.maximum(seg, partner)
    rows = 512

    def densify(b, carry):
        grp = b // 4
        row = b % 4
        acc[...] = jnp.zeros_like(acc)

        def slot(k, carry):
            j = (cols[grp, span, row, k] - 4 * (grp - 1) + 16) % 16
            acc[j] += a_all[grp, row, k].astype(jnp.float32)
            return carry

        lax.fori_loop(0, counts[grp, span, row], slot, 0)
        for j in range(12):
            dense[b, :, j * 128:(j + 1) * 128] = acc[j].astype(jnp.bfloat16)
        return carry

    lax.fori_loop(0, 16, densify, 0)

    def put(buf, grp, value):
        hid[buf, (grp + 1) * rows:(grp + 2) * rows, :] = value
        if grp == 3:
            hid[buf, 0:rows, :] = value
        if grp == 0:
            hid[buf, 5 * rows:6 * rows, :] = value

    for grp in range(4):
        put(0, grp, f_all[grp])

    def group_rows(l, grp, window):
        lhs = dense[pl.ds(grp * 4, 4)].reshape(rows, 12 * 128)
        agg = jnp.dot(lhs, window, preferred_element_type=jnp.float32)
        sup = (0.9 * agg + 0.1 * f_all[grp].astype(jnp.float32)).astype(jnp.bfloat16)
        branch = jnp.dot(sup, w_all[l], preferred_element_type=jnp.float32)
        beta = betas[l]
        res = (1.0 - beta) * sup.astype(jnp.float32) + beta * branch
        return jnp.maximum(res, 0.0).astype(jnp.bfloat16)

    def layer(l, carry):
        cur = l % 2
        for grp in range(4):
            put(1 - cur, grp, group_rows(l, grp, hid[cur, grp * rows:(grp + 3) * rows, :]))
        return carry

    lax.fori_loop(0, last - 1, layer, 0)
    cur = (last - 1) % 2
    low = hid[cur, pl.ds(pl.multiple_of((me + 1) * rows, rows), rows), :]
    for i in range(3):
        grp = (me + 3 + i) % 4
        window = hid[cur, pl.ds(pl.multiple_of(grp * rows, rows), 3 * rows), :]
        hid[1 - cur, i * rows:(i + 1) * rows, :] = group_rows(last - 1, grp, window)
    high = group_rows(last, me, hid[1 - cur, 0:3 * rows, :])

    @pl.when(seg == last)
    def _():
        own_out[...] = high
        other_out[...] = low

    @pl.when(seg != last)
    def _():
        own_out[...] = low
        other_out[...] = high


def whole_spans(features, tiles, tile_cols, tile_count, weights):
    seg = lax.axis_index("segment")
    span = (seg // 2) % 2
    any_spec = pl.BlockSpec(memory_space=pl.ANY)
    bf = jnp.bfloat16
    dma = pltpu.SemaphoreType.DMA
    a_all, f_all, c_all, n_all, w_all = pl.pallas_call(
        gather_kernel,
        out_shape=[
            jax.ShapeDtypeStruct((4,) + tiles.shape[1:], bf),
            jax.ShapeDtypeStruct((4,) + features.shape[1:], bf),
            jax.ShapeDtypeStruct((4,) + tile_cols.shape, jnp.int32),
            jax.ShapeDtypeStruct((4,) + tile_count.shape, jnp.int32),
            jax.ShapeDtypeStruct((8,) + weights.shape[1:], bf),
        ],
        in_specs=[any_spec] * 5,
        out_specs=[any_spec] * 5,
        scratch_shapes=[dma((5,)), dma((6, 2)), dma((6, 2)), dma((6, 2)), dma((6, 2)),
                        dma((3, 2)), dma((3, 2)), dma((3,)), dma((3,)), dma((4,)), dma((4,))],
        compiler_params=pltpu.CompilerParams(collective_id=0, has_side_effects=True),
        name="gather",
    )(tiles, features, tile_cols, tile_count, weights)
    betas = jnp.asarray(np.log(0.5 / (np.arange(8, dtype=np.float32) + 1.0) + 1.0), jnp.float32)
    smem = pl.BlockSpec(memory_space=pltpu.SMEM)
    vmem = pl.BlockSpec(memory_space=pltpu.VMEM)
    row_shape = jax.ShapeDtypeStruct(features.shape[1:], bf)
    own, other = pl.pallas_call(
        compute_kernel,
        out_shape=[row_shape, row_shape],
        in_specs=[smem, smem, smem, vmem, vmem, vmem],
        out_specs=[vmem, vmem],
        scratch_shapes=[pltpu.VMEM((16, 128, 1536), bf), pltpu.VMEM((12, 128, 128), jnp.float32),
                        pltpu.VMEM((2, 3072, 256), bf)],
        compiler_params=pltpu.CompilerParams(vmem_limit_bytes=48 * 1024 * 1024),
        name="layers",
    )(c_all, n_all, betas, a_all, f_all, w_all)
    other = lax.ppermute(other, "segment", [(s, s ^ 2) for s in range(8)])
    first = jnp.where(span == 0, own, other)
    second = jnp.where(span == 0, other, own)
    return jnp.stack([first, second])[None]


def solution(mesh):
    in_specs = (
        P(None, "node", None),
        P(None, "node", None, None, None),
        P(None, "node", None),
        P(None, "node"),
        P("segment", None, None),
    )
    out_specs = P("segment", None, "node", None)
    small = mesh.shape["segment"] == 8 and mesh.shape["node"] == 4
    return jax.shard_map(
        whole_spans if small else on_device, mesh=mesh, in_specs=in_specs, out_specs=out_specs, check_vma=False
    )
```

```python
import jax
import jax.numpy as jnp
import numpy as np
from jax import lax
from jax.experimental import pallas as pl
from jax.experimental.pallas import tpu as pltpu
from jax.sharding import PartitionSpec as P


def with_halo(array, sides, width):
    for axis, dim in sides:
        count, length = (lax.axis_size(axis), array.shape[dim])
        up = [(i, (i + 1) % count) for i in range(count)]
        down = [(j, i) for i, j in up]
        last = lax.slice_in_dim(array, length - width, length, axis=dim)
        first = lax.slice_in_dim(array, 0, width, axis=dim)
        before = lax.ppermute(last, axis, up)
        after = lax.ppermute(first, axis, down)
        array = jnp.concatenate([before, array, after], axis=dim)
    return array


def passed_along(block, axis, distance):
    devices = range(lax.axis_size(axis))
    route = [(i - distance, i) for i in devices if i - distance in devices]
    return lax.ppermute(block, axis, route)


def layer_rows(window, masked, columns, initial, weight, beta_mix):
    tile_size = masked.shape[-1]
    feature_width = window.shape[-1]
    grouped = window.reshape(window.shape[0] // tile_size, tile_size, feature_width)
    picked = grouped[columns]
    aggregate = jnp.einsum("bkij,bkjd->bid", masked, picked, preferred_element_type=jnp.float32)
    aggregate = aggregate.reshape(-1, feature_width)
    support = (0.9 * aggregate + 0.1 * initial.astype(jnp.float32)).astype(jnp.bfloat16)
    branch = jnp.dot(support, weight, preferred_element_type=jnp.float32)
    combined = (1.0 - beta_mix) * support.astype(jnp.float32) + beta_mix * branch
    return jnp.maximum(combined, 0.0).astype(jnp.bfloat16)


def on_device(features, tiles, tile_cols, tile_count, weights):
    segments = lax.axis_size("segment")
    groups = lax.axis_size("node")
    segment_id = lax.axis_index("segment")
    group_id = lax.axis_index("node")
    spans = features.shape[0]
    per_group = tiles.shape[1]
    total_blocks = per_group * groups
    first_block = (group_id - 1) * per_group
    local_cols = (tile_cols - first_block + total_blocks) % total_blocks
    slot_ids = jnp.arange(tiles.shape[2], dtype=jnp.int32)
    live = (slot_ids[None, None, :] < tile_count[:, :, None]).astype(jnp.bfloat16)
    masked = tiles * live[:, :, :, None, None]
    beta_mix = jnp.log(0.5 / (segment_id.astype(jnp.float32) + 1.0) + 1.0)
    weight = weights[0]
    rows_here = features.shape[1]

    def step(step_no, state_pair):
        incoming, stored = state_pair
        offset_now = step_no - segment_id
        active = (offset_now >= 0) & (offset_now < spans)
        span_id = jnp.clip(offset_now, 0, spans - 1)
        initial = lax.dynamic_index_in_dim(features, span_id, 0, keepdims=False)
        layer_input = jnp.where(segment_id == 0, initial, incoming)
        window = with_halo(layer_input, (("node", 0),), rows_here)
        span_tiles = lax.dynamic_index_in_dim(masked, span_id, 0, keepdims=False)
        span_cols = lax.dynamic_index_in_dim(local_cols, span_id, 0, keepdims=False)
        result = layer_rows(window, span_tiles, span_cols, initial, weight, beta_mix)
        updated = lax.dynamic_update_index_in_dim(stored, result, span_id, 0)
        stored = jnp.where(active, updated, stored)
        incoming = passed_along(result, "segment", 1)
        return (incoming, stored)

    start_pair = (
        jnp.zeros(features.shape[1:], jnp.bfloat16),
        jnp.zeros(features.shape, jnp.bfloat16),
    )
    final_pair = lax.fori_loop(0, segments + spans - 1, step, start_pair)
    stored = final_pair[1]
    return stored[None]


MESH = pl.DeviceIdType.MESH


def gather_kernel(tiles, cols, counts, a_all, c_all, n_all, loc_sem, ls, lr, cs, cr, ms, mr):
    seg = lax.axis_index("segment")
    g = lax.axis_index("node")
    c = seg % 2
    z = seg // 2
    span = z % 2
    xn = g + 1 - 2 * (g % 2)
    yn = (g + 2) % 4
    dn = 3 - g
    peer = seg + 1 - 2 * c

    barrier = pltpu.get_barrier_semaphore()
    for n in (xn, yn, dn):
        pl.semaphore_signal(barrier, inc=1, device_id={"node": n}, device_id_type=MESH)
    pl.semaphore_signal(barrier, inc=1, device_id={"segment": peer}, device_id_type=MESH)
    pl.semaphore_wait(barrier, 4)

    ln = xn * (1 - c) + yn * c
    on = yn * (1 - c) + xn * c

    def half(h):
        return pl.ds(h * 2, 2)

    def send(src, dst, idx, dev):
        on_link = idx < 3
        k = idx if on_link else idx - 3
        cp = pltpu.make_async_remote_copy(src, dst, (ls if on_link else cs).at[k], (lr if on_link else cr).at[k],
                                          device_id=dev, device_id_type=MESH)
        cp.start()
        return cp

    copies = []
    for i in range(2):
        h = half((i + c) % 2)
        copies.append(send(tiles.at[span, h], a_all.at[g, h], i, {"node": ln}))
    mcopies = []
    for d, n in enumerate((xn, yn, dn)):
        for k, (s, t) in enumerate(((cols, c_all), (counts, n_all))):
            cp = pltpu.make_async_remote_copy(s, t.at[g], ms.at[d, k], mr.at[d, k],
                                              device_id={"node": n}, device_id_type=MESH)
            cp.start()
            mcopies.append(cp)
    local = []
    for k, (s, t) in enumerate(((tiles.at[span], a_all.at[g]), (cols, c_all.at[g]), (counts, n_all.at[g]))):
        cp = pltpu.make_async_copy(s, t, loc_sem.at[k])
        cp.start()
        local.append(cp)

    share = []
    copies[0].wait_recv()
    p = a_all.at[ln, half(c)]
    share.append(send(p, p, 3, {"segment": peer}))
    share[0].wait_recv()
    p = a_all.at[on, half(1 - c)]
    copies.append(send(p, p, 2, {"node": ln}))
    copies[1].wait_recv()
    p = a_all.at[ln, half(1 - c)]
    share.append(send(p, p, 4, {"segment": peer}))
    copies[2].wait_recv()
    p = a_all.at[dn, half(1 - c)]
    share.append(send(p, p, 5, {"segment": peer}))
    share[1].wait_recv()
    share[2].wait_recv()
    for cp in mcopies:
        cp.wait()
    for cp in copies + share:
        cp.wait_send()
    for cp in local:
        cp.wait()


def compute_kernel(cols, counts, betas, a_all, f_all, w_all, own_out, other_out, dense, acc, hid, high_ref):
    seg = lax.axis_index("segment")
    me = lax.axis_index("node")
    c = seg % 2
    z = seg // 2
    span = z % 2
    partner = (z + 1 - 2 * span) * 2 + c
    last = jnp.maximum(seg, partner)
    rows = 512

    def densify(b, carry):
        grp = b // 4
        row = b % 4
        acc[...] = jnp.zeros_like(acc)

        def slot(k, carry):
            j = (cols[grp, span, row, k] - 4 * (grp - 1) + 16) % 16
            acc[j] += a_all[grp, row, k].astype(jnp.float32)
            return carry

        lax.fori_loop(0, counts[grp, span, row], slot, 0)
        for j in range(12):
            dense[b, :, j * 128:(j + 1) * 128] = acc[j].astype(jnp.bfloat16)
        return carry

    lax.fori_loop(0, 16, densify, 0)

    half = rows // 2

    def at(row):
        return pl.ds(pl.multiple_of(row, half), half)

    def put(buf, h, value):
        hid[buf, at(rows + h * half), :] = value

        @pl.when(h >= 6)
        def _():
            hid[buf, at((h - 6) * half), :] = value

        @pl.when(h < 2)
        def _():
            hid[buf, at((h + 10) * half), :] = value

    def start(h, carry):
        put(0, h, f_all[h // 2, at((h % 2) * half), :])
        return carry

    lax.fori_loop(0, 8, start, 0)

    def block_rows(l, h, window):
        lhs = dense[pl.ds(h * 2, 2)].reshape(half, 12 * 128)
        agg = jnp.dot(lhs, window, preferred_element_type=jnp.float32)
        first = f_all[h // 2, at((h % 2) * half), :]
        sup = (0.9 * agg + 0.1 * first.astype(jnp.float32)).astype(jnp.bfloat16)
        branch = jnp.dot(sup, w_all[l], preferred_element_type=jnp.float32)
        beta = betas[l]
        res = (1.0 - beta) * sup.astype(jnp.float32) + beta * branch
        return jnp.maximum(res, 0.0).astype(jnp.bfloat16)

    def window_of(cur, grp):
        return hid[cur, pl.ds(pl.multiple_of(grp * rows, rows), 3 * rows), :]

    def layer(l, carry):
        cur = l % 2

        def block(h, carry):
            put(1 - cur, h, block_rows(l, h, window_of(cur, h // 2)))
            return carry

        return lax.fori_loop(0, 8, block, carry)

    lax.fori_loop(0, last - 1, layer, 0)
    cur = (last - 1) % 2
    low_at = pl.ds(pl.multiple_of((me + 1) * rows, rows), rows)

    def block(i, carry):
        h = (2 * me + 6 + i) % 8
        hid[1 - cur, at(i * half), :] = block_rows(last - 1, h, window_of(cur, h // 2))
        return carry

    lax.fori_loop(0, 6, block, 0)
    low = hid[cur, low_at, :]

    def final(i, carry):
        high_ref[at(i * half), :] = block_rows(last, 2 * me + i, hid[1 - cur, 0:3 * rows, :])
        return carry

    lax.fori_loop(0, 2, final, 0)
    high = high_ref[...]

    @pl.when(seg == last)
    def _():
        own_out[...] = high
        other_out[...] = low

    @pl.when(seg != last)
    def _():
        own_out[...] = low
        other_out[...] = high


def whole_spans(features, tiles, tile_cols, tile_count, weights):
    seg = lax.axis_index("segment")
    span = (seg // 2) % 2
    any_spec = pl.BlockSpec(memory_space=pl.ANY)
    bf = jnp.bfloat16
    dma = pltpu.SemaphoreType.DMA
    w_all = lax.all_gather(weights[0], "segment")
    f_all = lax.all_gather(lax.dynamic_index_in_dim(features, span, 0, keepdims=False), "node")
    a_all, c_all, n_all = pl.pallas_call(
        gather_kernel,
        out_shape=[
            jax.ShapeDtypeStruct((4,) + tiles.shape[1:], bf),
            jax.ShapeDtypeStruct((4,) + tile_cols.shape, jnp.int32),
            jax.ShapeDtypeStruct((4,) + tile_count.shape, jnp.int32),
        ],
        in_specs=[any_spec] * 3,
        out_specs=[any_spec] * 3,
        scratch_shapes=[dma((3,)), dma((3,)), dma((3,)), dma((3,)), dma((3,)), dma((3, 2)), dma((3, 2))],
        compiler_params=pltpu.CompilerParams(collective_id=0, has_side_effects=True),
        cost_estimate=pl.CostEstimate(flops=0, bytes_accessed=100 * 1024 * 1024, transcendentals=0),
        name="gather",
    )(tiles, tile_cols, tile_count)
    betas = jnp.asarray(np.log(0.5 / (np.arange(8, dtype=np.float32) + 1.0) + 1.0), jnp.float32)
    smem = pl.BlockSpec(memory_space=pltpu.SMEM)
    vmem = pl.BlockSpec(memory_space=pltpu.VMEM)
    row_shape = jax.ShapeDtypeStruct(features.shape[1:], bf)
    own, other = pl.pallas_call(
        compute_kernel,
        out_shape=[row_shape, row_shape],
        in_specs=[smem, smem, smem, vmem, vmem, vmem],
        out_specs=[vmem, vmem],
        scratch_shapes=[pltpu.VMEM((16, 128, 1536), bf), pltpu.VMEM((12, 128, 128), jnp.float32),
                        pltpu.VMEM((2, 3072, 256), bf), pltpu.VMEM((512, 256), bf)],
        compiler_params=pltpu.CompilerParams(vmem_limit_bytes=48 * 1024 * 1024),
        name="layers",
    )(c_all, n_all, betas, a_all, f_all, w_all)
    other = lax.ppermute(other, "segment", [(s, s ^ 2) for s in range(8)])
    first = jnp.where(span == 0, own, other)
    second = jnp.where(span == 0, other, own)
    return jnp.stack([first, second])[None]


def solution(mesh):
    in_specs = (
        P(None, "node", None),
        P(None, "node", None, None, None),
        P(None, "node", None),
        P(None, "node"),
        P("segment", None, None),
    )
    out_specs = P("segment", None, "node", None)
    small = mesh.shape["segment"] == 8 and mesh.shape["node"] == 4
    return jax.shard_map(
        whole_spans if small else on_device, mesh=mesh, in_specs=in_specs, out_specs=out_specs, check_vma=False
    )
```

```python
import jax
import jax.numpy as jnp
import numpy as np
from jax import lax
from jax.experimental import pallas as pl
from jax.experimental.pallas import tpu as pltpu
from jax.sharding import PartitionSpec as P


def with_halo(array, sides, width):
    for axis, dim in sides:
        count, length = (lax.axis_size(axis), array.shape[dim])
        up = [(i, (i + 1) % count) for i in range(count)]
        down = [(j, i) for i, j in up]
        last = lax.slice_in_dim(array, length - width, length, axis=dim)
        first = lax.slice_in_dim(array, 0, width, axis=dim)
        before = lax.ppermute(last, axis, up)
        after = lax.ppermute(first, axis, down)
        array = jnp.concatenate([before, array, after], axis=dim)
    return array


def passed_along(block, axis, distance):
    devices = range(lax.axis_size(axis))
    route = [(i - distance, i) for i in devices if i - distance in devices]
    return lax.ppermute(block, axis, route)


def layer_rows(window, masked, columns, initial, weight, beta_mix):
    tile_size = masked.shape[-1]
    feature_width = window.shape[-1]
    grouped = window.reshape(window.shape[0] // tile_size, tile_size, feature_width)
    picked = grouped[columns]
    aggregate = jnp.einsum("bkij,bkjd->bid", masked, picked, preferred_element_type=jnp.float32)
    aggregate = aggregate.reshape(-1, feature_width)
    support = (0.9 * aggregate + 0.1 * initial.astype(jnp.float32)).astype(jnp.bfloat16)
    branch = jnp.dot(support, weight, preferred_element_type=jnp.float32)
    combined = (1.0 - beta_mix) * support.astype(jnp.float32) + beta_mix * branch
    return jnp.maximum(combined, 0.0).astype(jnp.bfloat16)


def on_device(features, tiles, tile_cols, tile_count, weights):
    segments = lax.axis_size("segment")
    groups = lax.axis_size("node")
    segment_id = lax.axis_index("segment")
    group_id = lax.axis_index("node")
    spans = features.shape[0]
    per_group = tiles.shape[1]
    total_blocks = per_group * groups
    first_block = (group_id - 1) * per_group
    local_cols = (tile_cols - first_block + total_blocks) % total_blocks
    slot_ids = jnp.arange(tiles.shape[2], dtype=jnp.int32)
    live = (slot_ids[None, None, :] < tile_count[:, :, None]).astype(jnp.bfloat16)
    masked = tiles * live[:, :, :, None, None]
    beta_mix = jnp.log(0.5 / (segment_id.astype(jnp.float32) + 1.0) + 1.0)
    weight = weights[0]
    rows_here = features.shape[1]

    def step(step_no, state_pair):
        incoming, stored = state_pair
        offset_now = step_no - segment_id
        active = (offset_now >= 0) & (offset_now < spans)
        span_id = jnp.clip(offset_now, 0, spans - 1)
        initial = lax.dynamic_index_in_dim(features, span_id, 0, keepdims=False)
        layer_input = jnp.where(segment_id == 0, initial, incoming)
        window = with_halo(layer_input, (("node", 0),), rows_here)
        span_tiles = lax.dynamic_index_in_dim(masked, span_id, 0, keepdims=False)
        span_cols = lax.dynamic_index_in_dim(local_cols, span_id, 0, keepdims=False)
        result = layer_rows(window, span_tiles, span_cols, initial, weight, beta_mix)
        updated = lax.dynamic_update_index_in_dim(stored, result, span_id, 0)
        stored = jnp.where(active, updated, stored)
        incoming = passed_along(result, "segment", 1)
        return (incoming, stored)

    start_pair = (
        jnp.zeros(features.shape[1:], jnp.bfloat16),
        jnp.zeros(features.shape, jnp.bfloat16),
    )
    final_pair = lax.fori_loop(0, segments + spans - 1, step, start_pair)
    stored = final_pair[1]
    return stored[None]


MESH = pl.DeviceIdType.MESH
ROWS = 512
WIDE = 12


def whole_kernel(betas, tiles, feats, cols, counts, weight, out,
                 a_all, f_all, c_vm, n_vm, c_all, n_all, w_all, dense, hid, own_ref, send_ref,
                 loc, asem, arec, fsem, frec, csem, crec, nsem, nrec, wsem, wrec, osem, orec):
    seg = lax.axis_index("segment")
    g = lax.axis_index("node")
    c = seg % 2
    z = seg // 2
    span = z % 2
    xn = g + 1 - 2 * (g % 2)
    yn = (g + 2) % 4
    dn = 3 - g
    partner = (z + 1 - 2 * span) * 2 + c
    last = seg + 2 - 2 * span

    def at(start, size):
        return pl.ds(pl.multiple_of(start, size), size)

    def remote(src, dst, ssem, rsem, dev):
        return pltpu.make_async_remote_copy(src, dst, ssem, rsem, device_id=dev, device_id_type=MESH)

    barrier = pltpu.get_barrier_semaphore()
    for n in (xn, yn, dn):
        pl.semaphore_signal(barrier, inc=1, device_id={"node": n}, device_id_type=MESH)
    for d in range(1, 8):
        pl.semaphore_signal(barrier, inc=1, device_id={"segment": (seg + d) % 8}, device_id_type=MESH)
    pl.semaphore_wait(barrier, 10)

    local = [pltpu.make_async_copy(s, t, loc.at[k]) for k, (s, t) in enumerate((
        (cols, c_vm.at[g]), (counts, n_vm.at[g]), (feats.at[span], f_all.at[g]),
        (tiles.at[span], a_all.at[g]), (weight.at[0], w_all.at[seg])))]
    for cp in local:
        cp.start()

    small = []
    for d, n in enumerate((xn, yn, dn)):
        small.append(remote(cols, c_vm.at[g], csem.at[d], crec.at[d], {"node": n}))
        small.append(remote(counts, n_vm.at[g], nsem.at[d], nrec.at[d], {"node": n}))
    first = [remote(feats.at[span], f_all.at[g], fsem.at[d], frec.at[d], {"node": n})
             for d, n in enumerate((xn, yn, dn))]
    for cp in small + first:
        cp.start()

    wcopies = [remote(weight.at[0], w_all.at[seg], wsem.at[d], wrec.at[d], {"segment": (seg + d + 1) % 8})
               for d in range(7)]

    @pl.when(z < 2)
    def _():
        for cp in wcopies:
            cp.start()

    def half(h):
        return pl.ds(h * 2, 2)

    def from_here(h, k, n):
        return remote(tiles.at[span, half(h)], a_all.at[g, half(h)], asem.at[k], arec.at[k], {"node": n})

    x0, y1, x1, y0 = from_here(0, 0, xn), from_here(1, 1, yn), from_here(1, 2, xn), from_here(0, 3, yn)
    for cp in (x0, y1, x1, y0):
        cp.start()

    for cp in local:
        cp.wait()
    for cp in small:
        cp.wait()
    meta = [pltpu.make_async_copy(c_vm, c_all, loc.at[0]), pltpu.make_async_copy(n_vm, n_all, loc.at[1])]
    for cp in meta:
        cp.start()
    for cp in meta:
        cp.wait()

    def densify(grp, h):
        def block(i, carry):
            row = h * 2 + i
            live = counts_of(grp, row)
            place = [(c_all[grp, span, row, k] - 4 * (grp - 1) + 16) % 16 for k in range(8)]
            place = [jnp.where(k < live, place[k], -1) for k in range(8)]

            def strip(r, carry):
                rows = at(r * 32, 32)
                part = [a_all[grp, row, k, rows, :].astype(jnp.float32) for k in range(8)]
                for j in range(WIDE):
                    total = None
                    for k in range(8):
                        term = part[k] * jnp.where(place[k] == j, 1.0, 0.0)
                        total = term if total is None else total + term
                    dense[grp * 4 + row, rows, j * 128:(j + 1) * 128] = total.astype(jnp.bfloat16)
                return carry

            return lax.fori_loop(0, 4, strip, carry)

        lax.fori_loop(0, 2, block, 0)

    def counts_of(grp, row):
        return n_all[grp, span, row]

    densify(g, 0)
    densify(g, 1)

    x0.wait_recv()
    xd = remote(a_all.at[xn, half(0)], a_all.at[xn, half(0)], asem.at[4], arec.at[4], {"node": yn})
    xd.start()
    y1.wait_recv()
    yd = remote(a_all.at[yn, half(1)], a_all.at[yn, half(1)], asem.at[5], arec.at[5], {"node": xn})
    yd.start()

    @pl.when(z >= 2)
    def _():
        for cp in wcopies:
            cp.start()

    densify(xn, 0)
    densify(yn, 1)

    def put(buf, grp, value):
        hid[buf, at((grp + 1) * ROWS, ROWS), :] = value

        @pl.when(grp == 3)
        def _():
            hid[buf, 0:ROWS, :] = value

        @pl.when(grp == 0)
        def _():
            hid[buf, 5 * ROWS:6 * ROWS, :] = value

    for cp in first:
        cp.wait()

    def start(grp, carry):
        put(0, grp, f_all[grp])
        return carry

    lax.fori_loop(0, 4, start, 0)
    x1.wait_recv()
    densify(xn, 1)
    y0.wait_recv()
    densify(yn, 0)
    xd.wait_recv()
    densify(dn, 0)
    yd.wait_recv()
    densify(dn, 1)
    for cp in (x0, y1, x1, y0, xd, yd):
        cp.wait_send()
    for cp in wcopies:
        cp.wait()

    def group_rows(l, grp, window):
        lhs = dense[pl.ds(grp * 4, 4)].reshape(ROWS, WIDE * 128)
        agg = jnp.dot(lhs, window, preferred_element_type=jnp.float32)
        sup = (0.9 * agg + 0.1 * f_all[grp].astype(jnp.float32)).astype(jnp.bfloat16)
        branch = jnp.dot(sup, w_all[l], preferred_element_type=jnp.float32)
        beta = betas[l]
        res = (1.0 - beta) * sup.astype(jnp.float32) + beta * branch
        return jnp.maximum(res, 0.0).astype(jnp.bfloat16)

    def window_of(buf, grp):
        return hid[buf, pl.ds(pl.multiple_of(grp * ROWS, ROWS), 3 * ROWS), :]

    def layer(l, carry):
        cur = l % 2

        def one(grp, carry):
            put(1 - cur, grp, group_rows(l, grp, window_of(cur, grp)))
            return carry

        return lax.fori_loop(0, 4, one, carry)

    lax.fori_loop(0, last - 1, layer, 0)
    cur = (last - 1) % 2
    low_at = at((g + 1) * ROWS, ROWS)
    across = remote(send_ref, out.at[0, span], osem, orec, {"segment": partner})

    @pl.when(span == 1)
    def _():
        send_ref[...] = hid[cur, low_at, :]
        across.start()

    @pl.when(span == 0)
    def _():
        own_ref[...] = hid[cur, low_at, :]

    def near(i, carry):
        grp = (g + 3 + i) % 4
        hid[1 - cur, at(i * ROWS, ROWS), :] = group_rows(last - 1, grp, window_of(cur, grp))
        return carry

    lax.fori_loop(0, 3, near, 0)
    high = group_rows(last, g, hid[1 - cur, 0:3 * ROWS, :])

    @pl.when(span == 0)
    def _():
        send_ref[...] = high
        across.start()

    @pl.when(span == 1)
    def _():
        own_ref[...] = high

    mine = pltpu.make_async_copy(own_ref, out.at[0, span], loc.at[0])
    mine.start()
    mine.wait()
    across.wait()


def whole_spans(features, tiles, tile_cols, tile_count, weights):
    any_spec = pl.BlockSpec(memory_space=pl.ANY)
    bf = jnp.bfloat16
    dma = pltpu.SemaphoreType.DMA
    betas = jnp.asarray(np.log(0.5 / (np.arange(8, dtype=np.float32) + 1.0) + 1.0), jnp.float32)
    width = features.shape[-1]
    return pl.pallas_call(
        whole_kernel,
        out_shape=jax.ShapeDtypeStruct((1,) + features.shape, bf),
        in_specs=[pl.BlockSpec(memory_space=pltpu.SMEM)] + [any_spec] * 5,
        out_specs=any_spec,
        scratch_shapes=[
            pltpu.VMEM((4,) + tiles.shape[1:], bf),
            pltpu.VMEM((4,) + features.shape[1:], bf),
            pltpu.VMEM((4,) + tile_cols.shape, jnp.int32),
            pltpu.VMEM((4,) + tile_count.shape, jnp.int32),
            pltpu.SMEM((4,) + tile_cols.shape, jnp.int32),
            pltpu.SMEM((4,) + tile_count.shape, jnp.int32),
            pltpu.VMEM((8,) + weights.shape[1:], bf),
            pltpu.VMEM((16, 128, WIDE * 128), bf),
            pltpu.VMEM((2, 6 * ROWS, width), bf),
            pltpu.VMEM((ROWS, width), bf),
            pltpu.VMEM((ROWS, width), bf),
            dma((5,)), dma((6,)), dma((6,)), dma((3,)), dma((3,)), dma((3,)), dma((3,)),
            dma((3,)), dma((3,)), dma((7,)), dma((7,)), dma, dma,
        ],
        compiler_params=pltpu.CompilerParams(collective_id=0, has_side_effects=True,
                                             vmem_limit_bytes=48 * 1024 * 1024),
        cost_estimate=pl.CostEstimate(flops=15_000_000_000, bytes_accessed=8_000_000, transcendentals=0),
        name="whole",
    )(betas, tiles, features, tile_cols, tile_count, weights)


def solution(mesh):
    in_specs = (
        P(None, "node", None),
        P(None, "node", None, None, None),
        P(None, "node", None),
        P(None, "node"),
        P("segment", None, None),
    )
    out_specs = P("segment", None, "node", None)
    small = mesh.shape["segment"] == 8 and mesh.shape["node"] == 4
    return jax.shard_map(
        whole_spans if small else on_device, mesh=mesh, in_specs=in_specs, out_specs=out_specs, check_vma=False
    )
```

```python
import jax
import jax.numpy as jnp
import numpy as np
from jax import lax
from jax.experimental import pallas as pl
from jax.experimental.pallas import tpu as pltpu
from jax.sharding import PartitionSpec as P


def with_halo(array, sides, width):
    for axis, dim in sides:
        count, length = (lax.axis_size(axis), array.shape[dim])
        up = [(i, (i + 1) % count) for i in range(count)]
        down = [(j, i) for i, j in up]
        last = lax.slice_in_dim(array, length - width, length, axis=dim)
        first = lax.slice_in_dim(array, 0, width, axis=dim)
        before = lax.ppermute(last, axis, up)
        after = lax.ppermute(first, axis, down)
        array = jnp.concatenate([before, array, after], axis=dim)
    return array


def passed_along(block, axis, distance):
    devices = range(lax.axis_size(axis))
    route = [(i - distance, i) for i in devices if i - distance in devices]
    return lax.ppermute(block, axis, route)


def layer_rows(window, masked, columns, initial, weight, beta_mix):
    tile_size = masked.shape[-1]
    feature_width = window.shape[-1]
    grouped = window.reshape(window.shape[0] // tile_size, tile_size, feature_width)
    picked = grouped[columns]
    aggregate = jnp.einsum("bkij,bkjd->bid", masked, picked, preferred_element_type=jnp.float32)
    aggregate = aggregate.reshape(-1, feature_width)
    support = (0.9 * aggregate + 0.1 * initial.astype(jnp.float32)).astype(jnp.bfloat16)
    branch = jnp.dot(support, weight, preferred_element_type=jnp.float32)
    combined = (1.0 - beta_mix) * support.astype(jnp.float32) + beta_mix * branch
    return jnp.maximum(combined, 0.0).astype(jnp.bfloat16)


def on_device(features, tiles, tile_cols, tile_count, weights):
    segments = lax.axis_size("segment")
    groups = lax.axis_size("node")
    segment_id = lax.axis_index("segment")
    group_id = lax.axis_index("node")
    spans = features.shape[0]
    per_group = tiles.shape[1]
    total_blocks = per_group * groups
    first_block = (group_id - 1) * per_group
    local_cols = (tile_cols - first_block + total_blocks) % total_blocks
    slot_ids = jnp.arange(tiles.shape[2], dtype=jnp.int32)
    live = (slot_ids[None, None, :] < tile_count[:, :, None]).astype(jnp.bfloat16)
    masked = tiles * live[:, :, :, None, None]
    beta_mix = jnp.log(0.5 / (segment_id.astype(jnp.float32) + 1.0) + 1.0)
    weight = weights[0]
    rows_here = features.shape[1]

    def step(step_no, state_pair):
        incoming, stored = state_pair
        offset_now = step_no - segment_id
        active = (offset_now >= 0) & (offset_now < spans)
        span_id = jnp.clip(offset_now, 0, spans - 1)
        initial = lax.dynamic_index_in_dim(features, span_id, 0, keepdims=False)
        layer_input = jnp.where(segment_id == 0, initial, incoming)
        window = with_halo(layer_input, (("node", 0),), rows_here)
        span_tiles = lax.dynamic_index_in_dim(masked, span_id, 0, keepdims=False)
        span_cols = lax.dynamic_index_in_dim(local_cols, span_id, 0, keepdims=False)
        result = layer_rows(window, span_tiles, span_cols, initial, weight, beta_mix)
        updated = lax.dynamic_update_index_in_dim(stored, result, span_id, 0)
        stored = jnp.where(active, updated, stored)
        incoming = passed_along(result, "segment", 1)
        return (incoming, stored)

    start_pair = (
        jnp.zeros(features.shape[1:], jnp.bfloat16),
        jnp.zeros(features.shape, jnp.bfloat16),
    )
    final_pair = lax.fori_loop(0, segments + spans - 1, step, start_pair)
    stored = final_pair[1]
    return stored[None]


MESH = pl.DeviceIdType.MESH
ROWS = 512
WIDE = 12


def whole_kernel(betas, tiles, feats, cols, counts, weight, out,
                 a_all, f_all, c_vm, n_vm, c_all, n_all, w_all, dense, hid, own_ref, send_ref,
                 loc, asem, arec, fsem, frec, csem, crec, nsem, nrec, wsem, wrec, osem, orec):
    seg = lax.axis_index("segment")
    g = lax.axis_index("node")
    c = seg % 2
    z = seg // 2
    span = z % 2
    xn = g + 1 - 2 * (g % 2)
    yn = (g + 2) % 4
    dn = 3 - g
    partner = (z + 1 - 2 * span) * 2 + c
    last = seg + 2 - 2 * span

    def at(start, size):
        return pl.ds(pl.multiple_of(start, size), size)

    def remote(src, dst, ssem, rsem, dev):
        return pltpu.make_async_remote_copy(src, dst, ssem, rsem, device_id=dev, device_id_type=MESH)

    barrier = pltpu.get_barrier_semaphore()
    for n in (xn, yn, dn):
        pl.semaphore_signal(barrier, inc=1, device_id={"node": n}, device_id_type=MESH)
    for d in range(1, 8):
        pl.semaphore_signal(barrier, inc=1, device_id={"segment": (seg + d) % 8}, device_id_type=MESH)
    pl.semaphore_wait(barrier, 10)

    local = [pltpu.make_async_copy(s, t, loc.at[k]) for k, (s, t) in enumerate((
        (cols, c_vm.at[g]), (counts, n_vm.at[g]), (feats.at[span], f_all.at[g]),
        (tiles.at[span], a_all.at[g]), (weight.at[0], w_all.at[seg])))]
    for cp in local:
        cp.start()

    small = []
    for d, n in enumerate((xn, yn, dn)):
        small.append(remote(cols, c_vm.at[g], csem.at[d], crec.at[d], {"node": n}))
        small.append(remote(counts, n_vm.at[g], nsem.at[d], nrec.at[d], {"node": n}))
    first = [remote(feats.at[span], f_all.at[g], fsem.at[d], frec.at[d], {"node": n})
             for d, n in enumerate((xn, yn, dn))]
    for cp in small + first:
        cp.start()

    low_copies = [remote(weight.at[0], w_all.at[seg], wsem.at[d], wrec.at[seg], {"segment": (seg + d + 1) % 8})
                  for d in range(7)]
    high_copies = [remote(weight.at[0], w_all.at[seg], wsem.at[d], wrec.at[seg], {"segment": 4 + (seg + d + 1) % 4})
                   for d in range(3)]

    @pl.when(z < 2)
    def _():
        for cp in low_copies:
            cp.start()

    def half(h):
        return pl.ds(h * 2, 2)

    def from_here(h, k, n):
        return remote(tiles.at[span, half(h)], a_all.at[g, half(h)], asem.at[k], arec.at[k], {"node": n})

    x0, y1, x1, y0 = from_here(0, 0, xn), from_here(1, 1, yn), from_here(1, 2, xn), from_here(0, 3, yn)
    for cp in (x0, y1, x1, y0):
        cp.start()

    @pl.when(z >= 2)
    def _():
        for cp in high_copies:
            cp.start()

    for cp in local:
        cp.wait()
    for cp in small:
        cp.wait()
    meta = [pltpu.make_async_copy(c_vm, c_all, loc.at[0]), pltpu.make_async_copy(n_vm, n_all, loc.at[1])]
    for cp in meta:
        cp.start()
    for cp in meta:
        cp.wait()

    def densify(grp, h):
        def block(i, carry):
            row = h * 2 + i
            live = counts_of(grp, row)
            place = [(c_all[grp, span, row, k] - 4 * (grp - 1) + 16) % 16 for k in range(8)]
            place = [jnp.where(k < live, place[k], -1) for k in range(8)]

            def strip(r, carry):
                rows = at(r * 32, 32)
                part = [a_all[grp, row, k, rows, :].astype(jnp.float32) for k in range(8)]
                for j in range(WIDE):
                    total = None
                    for k in range(8):
                        term = part[k] * jnp.where(place[k] == j, 1.0, 0.0)
                        total = term if total is None else total + term
                    dense[grp * 4 + row, rows, j * 128:(j + 1) * 128] = total.astype(jnp.bfloat16)
                return carry

            return lax.fori_loop(0, 4, strip, carry)

        lax.fori_loop(0, 2, block, 0)

    def counts_of(grp, row):
        return n_all[grp, span, row]

    densify(g, 0)
    densify(g, 1)

    via = xn * (1 - c) + yn * c
    beyond = yn * (1 - c) + xn * c
    peer = seg + 1 - 2 * c
    arrived_at = remote(tiles.at[span, half(0)], a_all.at[g, half(0)], asem.at[c], arec.at[c], {"node": xn})
    other_at = remote(tiles.at[span, half(0)], a_all.at[g, half(0)], asem.at[1 - c], arec.at[1 - c], {"node": xn})
    arrived_at.wait_recv()
    onward = [remote(a_all.at[via, 2 * c + i], a_all.at[via, 2 * c + i], asem.at[4 + i], arec.at[4 + i],
                     {"node": beyond}) for i in range(2)]
    for cp in onward:
        cp.start()
    other_at.wait_recv()
    densify(xn, 0)
    densify(yn, 1)

    def put(buf, grp, value):
        hid[buf, at((grp + 1) * ROWS, ROWS), :] = value

        @pl.when(grp == 3)
        def _():
            hid[buf, 0:ROWS, :] = value

        @pl.when(grp == 0)
        def _():
            hid[buf, 5 * ROWS:6 * ROWS, :] = value

    for cp in first:
        cp.wait()

    def start(grp, carry):
        put(0, grp, f_all[grp])
        return carry

    lax.fori_loop(0, 4, start, 0)
    x1.wait_recv()
    densify(xn, 1)
    y0.wait_recv()
    densify(yn, 0)
    shares = []
    for i in range(2):
        onward[i].wait_recv()
        p = a_all.at[dn, 2 * c + i]
        shares.append(remote(p, p, asem.at[6 + i], arec.at[6 + i], {"segment": peer}))
        shares[i].start()

    def weight_here(l):
        @pl.when(l != seg)
        def _():
            remote(weight.at[0], w_all.at[l], wsem.at[0], wrec.at[l], {"segment": peer}).wait_recv()

    def group_rows(l, grp, window):
        lhs = dense[pl.ds(grp * 4, 4)].reshape(ROWS, WIDE * 128)
        agg = jnp.dot(lhs, window, preferred_element_type=jnp.float32)
        sup = (0.9 * agg + 0.1 * f_all[grp].astype(jnp.float32)).astype(jnp.bfloat16)
        branch = jnp.dot(sup, w_all[l], preferred_element_type=jnp.float32)
        beta = betas[l]
        res = (1.0 - beta) * sup.astype(jnp.float32) + beta * branch
        return jnp.maximum(res, 0.0).astype(jnp.bfloat16)

    def window_of(buf, grp):
        return hid[buf, pl.ds(pl.multiple_of(grp * ROWS, ROWS), 3 * ROWS), :]

    def layer(l, carry):
        cur = l % 2
        weight_here(l)

        def one(grp, carry):
            put(1 - cur, grp, group_rows(l, grp, window_of(cur, grp)))
            return carry

        return lax.fori_loop(0, 4, one, carry)

    weight_here(0)

    def early(i, carry):
        grp = (dn + 1 + i) % 4
        put(1, grp, group_rows(0, grp, window_of(0, grp)))
        return carry

    lax.fori_loop(0, 3, early, 0)
    densify(dn, c)
    for cp in shares:
        cp.wait_recv()
    densify(dn, 1 - c)
    put(1, dn, group_rows(0, dn, window_of(0, dn)))
    lax.fori_loop(1, last - 1, layer, 0)
    cur = (last - 1) % 2
    low_at = at((g + 1) * ROWS, ROWS)
    across = remote(send_ref, out.at[0, span], osem, orec, {"segment": partner})

    @pl.when(span == 1)
    def _():
        send_ref[...] = hid[cur, low_at, :]
        across.start()

    @pl.when(span == 0)
    def _():
        own_ref[...] = hid[cur, low_at, :]

    weight_here(last - 1)

    def near(i, carry):
        grp = (g + 3 + i) % 4
        hid[1 - cur, at(i * ROWS, ROWS), :] = group_rows(last - 1, grp, window_of(cur, grp))
        return carry

    lax.fori_loop(0, 3, near, 0)
    weight_here(last)
    high = group_rows(last, g, hid[1 - cur, 0:3 * ROWS, :])

    @pl.when(span == 0)
    def _():
        send_ref[...] = high
        across.start()

    @pl.when(span == 1)
    def _():
        own_ref[...] = high

    mine = pltpu.make_async_copy(own_ref, out.at[0, span], loc.at[0])
    mine.start()

    def rest(l, carry):
        weight_here(l)
        return carry

    lax.fori_loop(last + 1, jnp.where(z < 2, 4, 8), rest, 0)
    for cp in [x0, y1, x1, y0] + onward + shares:
        cp.wait_send()

    @pl.when(z < 2)
    def _():
        for cp in low_copies:
            cp.wait_send()

    @pl.when(z >= 2)
    def _():
        for cp in high_copies:
            cp.wait_send()

    mine.wait()
    across.wait()


def whole_spans(features, tiles, tile_cols, tile_count, weights):
    hbm = pl.BlockSpec(memory_space=pltpu.HBM)
    bf = jnp.bfloat16
    dma = pltpu.SemaphoreType.DMA
    betas = jnp.asarray(np.log(0.5 / (np.arange(8, dtype=np.float32) + 1.0) + 1.0), jnp.float32)
    width = features.shape[-1]
    return pl.pallas_call(
        whole_kernel,
        out_shape=jax.ShapeDtypeStruct((1,) + features.shape, bf),
        in_specs=[pl.BlockSpec(memory_space=pltpu.SMEM)] + [hbm] * 5,
        out_specs=hbm,
        scratch_shapes=[
            pltpu.VMEM((4,) + tiles.shape[1:], bf),
            pltpu.VMEM((4,) + features.shape[1:], bf),
            pltpu.VMEM((4,) + tile_cols.shape, jnp.int32),
            pltpu.VMEM((4,) + tile_count.shape, jnp.int32),
            pltpu.SMEM((4,) + tile_cols.shape, jnp.int32),
            pltpu.SMEM((4,) + tile_count.shape, jnp.int32),
            pltpu.VMEM((8,) + weights.shape[1:], bf),
            pltpu.VMEM((16, 128, WIDE * 128), bf),
            pltpu.VMEM((2, 6 * ROWS, width), bf),
            pltpu.VMEM((ROWS, width), bf),
            pltpu.VMEM((ROWS, width), bf),
            dma((5,)), dma((8,)), dma((8,)), dma((3,)), dma((3,)), dma((3,)), dma((3,)),
            dma((3,)), dma((3,)), dma((7,)), dma((8,)), dma, dma,
        ],
        compiler_params=pltpu.CompilerParams(collective_id=0, has_side_effects=True,
                                             vmem_limit_bytes=63 * 1024 * 1024),
        cost_estimate=pl.CostEstimate(flops=15_000_000_000, bytes_accessed=8_000_000, transcendentals=0),
        name="whole",
    )(betas, tiles, features, tile_cols, tile_count, weights)


def solution(mesh):
    in_specs = (
        P(None, "node", None),
        P(None, "node", None, None, None),
        P(None, "node", None),
        P(None, "node"),
        P("segment", None, None),
    )
    out_specs = P("segment", None, "node", None)
    small = mesh.shape["segment"] == 8 and mesh.shape["node"] == 4
    return jax.shard_map(
        whole_spans if small else on_device, mesh=mesh, in_specs=in_specs, out_specs=out_specs, check_vma=False
    )
```

```python
import jax
import jax.numpy as jnp
import numpy as np
from jax import lax
from jax.experimental import pallas as pl
from jax.experimental.pallas import tpu as pltpu
from jax.sharding import PartitionSpec as P


def with_halo(array, sides, width):
    for axis, dim in sides:
        count, length = (lax.axis_size(axis), array.shape[dim])
        up = [(i, (i + 1) % count) for i in range(count)]
        down = [(j, i) for i, j in up]
        last = lax.slice_in_dim(array, length - width, length, axis=dim)
        first = lax.slice_in_dim(array, 0, width, axis=dim)
        before = lax.ppermute(last, axis, up)
        after = lax.ppermute(first, axis, down)
        array = jnp.concatenate([before, array, after], axis=dim)
    return array


def passed_along(block, axis, distance):
    devices = range(lax.axis_size(axis))
    route = [(i - distance, i) for i in devices if i - distance in devices]
    return lax.ppermute(block, axis, route)


def layer_rows(window, masked, columns, initial, weight, beta_mix):
    tile_size = masked.shape[-1]
    feature_width = window.shape[-1]
    grouped = window.reshape(window.shape[0] // tile_size, tile_size, feature_width)
    picked = grouped[columns]
    aggregate = jnp.einsum("bkij,bkjd->bid", masked, picked, preferred_element_type=jnp.float32)
    aggregate = aggregate.reshape(-1, feature_width)
    support = (0.9 * aggregate + 0.1 * initial.astype(jnp.float32)).astype(jnp.bfloat16)
    branch = jnp.dot(support, weight, preferred_element_type=jnp.float32)
    combined = (1.0 - beta_mix) * support.astype(jnp.float32) + beta_mix * branch
    return jnp.maximum(combined, 0.0).astype(jnp.bfloat16)


def on_device(features, tiles, tile_cols, tile_count, weights):
    segments = lax.axis_size("segment")
    groups = lax.axis_size("node")
    segment_id = lax.axis_index("segment")
    group_id = lax.axis_index("node")
    spans = features.shape[0]
    per_group = tiles.shape[1]
    total_blocks = per_group * groups
    first_block = (group_id - 1) * per_group
    local_cols = (tile_cols - first_block + total_blocks) % total_blocks
    slot_ids = jnp.arange(tiles.shape[2], dtype=jnp.int32)
    live = (slot_ids[None, None, :] < tile_count[:, :, None]).astype(jnp.bfloat16)
    masked = tiles * live[:, :, :, None, None]
    beta_mix = jnp.log(0.5 / (segment_id.astype(jnp.float32) + 1.0) + 1.0)
    weight = weights[0]
    rows_here = features.shape[1]

    def step(step_no, state_pair):
        incoming, stored = state_pair
        offset_now = step_no - segment_id
        active = (offset_now >= 0) & (offset_now < spans)
        span_id = jnp.clip(offset_now, 0, spans - 1)
        initial = lax.dynamic_index_in_dim(features, span_id, 0, keepdims=False)
        layer_input = jnp.where(segment_id == 0, initial, incoming)
        window = with_halo(layer_input, (("node", 0),), rows_here)
        span_tiles = lax.dynamic_index_in_dim(masked, span_id, 0, keepdims=False)
        span_cols = lax.dynamic_index_in_dim(local_cols, span_id, 0, keepdims=False)
        result = layer_rows(window, span_tiles, span_cols, initial, weight, beta_mix)
        updated = lax.dynamic_update_index_in_dim(stored, result, span_id, 0)
        stored = jnp.where(active, updated, stored)
        incoming = passed_along(result, "segment", 1)
        return (incoming, stored)

    start_pair = (
        jnp.zeros(features.shape[1:], jnp.bfloat16),
        jnp.zeros(features.shape, jnp.bfloat16),
    )
    final_pair = lax.fori_loop(0, segments + spans - 1, step, start_pair)
    stored = final_pair[1]
    return stored[None]


MESH = pl.DeviceIdType.MESH
ROWS = 512
WIDE = 12


def whole_kernel(betas, tiles, feats, cols, counts, weight, out,
                 a_all, f_all, c_vm, n_vm, c_all, n_all, w_all, dense, hid, own_ref, send_ref,
                 loc, asem, arec, fsem, frec, csem, crec, nsem, nrec, wsem, wrec, osem, orec):
    seg = lax.axis_index("segment")
    g = lax.axis_index("node")
    c = seg % 2
    z = seg // 2
    span = z % 2
    xn = g + 1 - 2 * (g % 2)
    yn = (g + 2) % 4
    dn = 3 - g
    partner = (z + 1 - 2 * span) * 2 + c
    last = seg + 2 - 2 * span

    def at(start, size):
        return pl.ds(pl.multiple_of(start, size), size)

    def remote(src, dst, ssem, rsem, dev):
        return pltpu.make_async_remote_copy(src, dst, ssem, rsem, device_id=dev, device_id_type=MESH)

    barrier = pltpu.get_barrier_semaphore()
    for n in (xn, yn, dn):
        pl.semaphore_signal(barrier, inc=1, device_id={"node": n}, device_id_type=MESH)
    for d in range(1, 8):
        pl.semaphore_signal(barrier, inc=1, device_id={"segment": (seg + d) % 8}, device_id_type=MESH)
    pl.semaphore_wait(barrier, 10)

    local = [pltpu.make_async_copy(s, t, loc.at[k]) for k, (s, t) in enumerate((
        (cols, c_vm.at[g]), (counts, n_vm.at[g]), (feats.at[span], f_all.at[g]),
        (tiles.at[span], a_all.at[g]), (weight.at[0], w_all.at[seg])))]
    for cp in local:
        cp.start()

    small = []
    for d, n in enumerate((xn, yn, dn)):
        small.append(remote(cols, c_vm.at[g], csem.at[d], crec.at[d], {"node": n}))
        small.append(remote(counts, n_vm.at[g], nsem.at[d], nrec.at[d], {"node": n}))
    first = [remote(feats.at[span], f_all.at[g], fsem.at[d], frec.at[d], {"node": n})
             for d, n in enumerate((xn, yn))]
    part = at(c * 256, 256)
    first.append(remote(feats.at[span, part], f_all.at[g, part], fsem.at[2], frec.at[2], {"node": dn}))
    for cp in small + first:
        cp.start()

    low_copies = [remote(weight.at[0], w_all.at[seg], wsem.at[d], wrec.at[seg], {"segment": (seg + d + 1) % 8})
                  for d in range(7)]
    high_copies = [remote(weight.at[0], w_all.at[seg], wsem.at[d], wrec.at[seg], {"segment": 4 + (seg + d + 1) % 4})
                   for d in range(3)]

    @pl.when(z < 2)
    def _():
        for cp in low_copies:
            cp.start()

    front = pl.ds(2 * c, 2)
    inner = pl.ds(2 - c, 1)
    direct = [remote(tiles.at[span, rows], a_all.at[g, rows], asem.at[k], arec.at[k], {"node": n})
              for k, (rows, n) in enumerate(((front, xn), (front, yn), (inner, xn), (inner, yn)))]
    for cp in direct:
        cp.start()

    @pl.when(z >= 2)
    def _():
        for cp in high_copies:
            cp.start()

    for cp in local:
        cp.wait()
    for cp in small:
        cp.wait()
    meta = [pltpu.make_async_copy(c_vm, c_all, loc.at[0]), pltpu.make_async_copy(n_vm, n_all, loc.at[1])]
    for cp in meta:
        cp.start()
    for cp in meta:
        cp.wait()

    def densify(grp, from_row, count):
        def block(i, carry):
            row = from_row + i
            live = counts_of(grp, row)
            place = [(c_all[grp, span, row, k] - 4 * (grp - 1) + 16) % 16 for k in range(8)]
            place = [jnp.where(k < live, place[k], -1) for k in range(8)]

            def strip(r, carry):
                rows = at(r * 32, 32)
                part = [a_all[grp, row, k, rows, :].astype(jnp.float32) for k in range(8)]
                for j in range(WIDE):
                    total = None
                    for k in range(8):
                        term = part[k] * jnp.where(place[k] == j, 1.0, 0.0)
                        total = term if total is None else total + term
                    dense[grp * 4 + row, rows, j * 128:(j + 1) * 128] = total.astype(jnp.bfloat16)
                return carry

            return lax.fori_loop(0, 4, strip, carry)

        lax.fori_loop(0, count, block, 0)

    def counts_of(grp, row):
        return n_all[grp, span, row]

    densify(g, 0, 4)

    via = xn * (1 - c) + yn * c
    beyond = yn * (1 - c) + xn * c
    peer = seg + 1 - 2 * c

    def across_chip(piece, k):
        return remote(piece, piece, asem.at[k], arec.at[k], {"segment": peer})

    for cp in first:
        cp.wait_recv()
    first_share = across_chip(f_all.at[dn, part], 10)
    first_share.start()
    for k in (c, 1 - c):
        remote(tiles.at[span, front], a_all.at[g, front], asem.at[k], arec.at[k], {"node": xn}).wait_recv()
        if k is c:
            onward = [remote(a_all.at[via, 2 * c + i], a_all.at[via, 2 * c + i], asem.at[4 + i], arec.at[4 + i],
                             {"node": beyond}) for i in range(2)]
            for cp in onward:
                cp.start()
    edge = [across_chip(a_all.at[n, 3 * c], 8 + k) for k, n in enumerate((xn, yn))]
    for cp in edge:
        cp.start()
    densify(xn, 2 * c, 2)
    densify(yn, 2 * c, 2)

    def put(buf, grp, value):
        hid[buf, at((grp + 1) * ROWS, ROWS), :] = value

        @pl.when(grp == 3)
        def _():
            hid[buf, 0:ROWS, :] = value

        @pl.when(grp == 0)
        def _():
            hid[buf, 5 * ROWS:6 * ROWS, :] = value

    first_share.wait_recv()

    def start(grp, carry):
        put(0, grp, f_all[grp])
        return carry

    lax.fori_loop(0, 4, start, 0)
    direct[2].wait_recv()
    densify(xn, 2 - c, 1)
    direct[3].wait_recv()
    densify(yn, 2 - c, 1)
    edge[0].wait_recv()
    densify(xn, 3 - 3 * c, 1)
    edge[1].wait_recv()
    densify(yn, 3 - 3 * c, 1)
    shares = []
    for i in range(2):
        onward[i].wait_recv()
        p = a_all.at[dn, 2 * c + i]
        shares.append(remote(p, p, asem.at[6 + i], arec.at[6 + i], {"segment": peer}))
        shares[i].start()

    def weight_here(l):
        @pl.when(l != seg)
        def _():
            remote(weight.at[0], w_all.at[l], wsem.at[0], wrec.at[l], {"segment": peer}).wait_recv()

    def group_rows(l, grp, window):
        lhs = dense[pl.ds(grp * 4, 4)].reshape(ROWS, WIDE * 128)
        agg = jnp.dot(lhs, window, preferred_element_type=jnp.float32)
        sup = (0.9 * agg + 0.1 * f_all[grp].astype(jnp.float32)).astype(jnp.bfloat16)
        branch = jnp.dot(sup, w_all[l], preferred_element_type=jnp.float32)
        beta = betas[l]
        res = (1.0 - beta) * sup.astype(jnp.float32) + beta * branch
        return jnp.maximum(res, 0.0).astype(jnp.bfloat16)

    def window_of(buf, grp):
        return hid[buf, pl.ds(pl.multiple_of(grp * ROWS, ROWS), 3 * ROWS), :]

    def layer(l, carry):
        cur = l % 2
        weight_here(l)

        def one(grp, carry):
            put(1 - cur, grp, group_rows(l, grp, window_of(cur, grp)))
            return carry

        return lax.fori_loop(0, 4, one, carry)

    weight_here(0)

    def early(i, carry):
        grp = (dn + 1 + i) % 4
        put(1, grp, group_rows(0, grp, window_of(0, grp)))
        return carry

    lax.fori_loop(0, 3, early, 0)
    densify(dn, 2 * c, 2)
    for cp in shares:
        cp.wait_recv()
    densify(dn, 2 - 2 * c, 2)
    put(1, dn, group_rows(0, dn, window_of(0, dn)))
    lax.fori_loop(1, last - 1, layer, 0)
    cur = (last - 1) % 2
    low_at = at((g + 1) * ROWS, ROWS)
    across = remote(send_ref, out.at[0, span], osem, orec, {"segment": partner})

    @pl.when(span == 1)
    def _():
        send_ref[...] = hid[cur, low_at, :]
        across.start()

    @pl.when(span == 0)
    def _():
        own_ref[...] = hid[cur, low_at, :]

    weight_here(last - 1)

    def near(i, carry):
        grp = (g + 3 + i) % 4
        hid[1 - cur, at(i * ROWS, ROWS), :] = group_rows(last - 1, grp, window_of(cur, grp))
        return carry

    lax.fori_loop(0, 3, near, 0)
    weight_here(last)
    high = group_rows(last, g, hid[1 - cur, 0:3 * ROWS, :])

    @pl.when(span == 0)
    def _():
        send_ref[...] = high
        across.start()

    @pl.when(span == 1)
    def _():
        own_ref[...] = high

    mine = pltpu.make_async_copy(own_ref, out.at[0, span], loc.at[0])
    mine.start()

    def rest(l, carry):
        weight_here(l)
        return carry

    lax.fori_loop(last + 1, jnp.where(z < 2, 4, 8), rest, 0)
    for cp in direct + onward + shares + edge + first + [first_share]:
        cp.wait_send()

    @pl.when(z < 2)
    def _():
        for cp in low_copies:
            cp.wait_send()

    @pl.when(z >= 2)
    def _():
        for cp in high_copies:
            cp.wait_send()

    mine.wait()
    across.wait()


def whole_spans(features, tiles, tile_cols, tile_count, weights):
    hbm = pl.BlockSpec(memory_space=pltpu.HBM)
    bf = jnp.bfloat16
    dma = pltpu.SemaphoreType.DMA
    betas = jnp.asarray(np.log(0.5 / (np.arange(8, dtype=np.float32) + 1.0) + 1.0), jnp.float32)
    width = features.shape[-1]
    return pl.pallas_call(
        whole_kernel,
        out_shape=jax.ShapeDtypeStruct((1,) + features.shape, bf),
        in_specs=[pl.BlockSpec(memory_space=pltpu.SMEM)] + [hbm] * 5,
        out_specs=hbm,
        scratch_shapes=[
            pltpu.VMEM((4,) + tiles.shape[1:], bf),
            pltpu.VMEM((4,) + features.shape[1:], bf),
            pltpu.VMEM((4,) + tile_cols.shape, jnp.int32),
            pltpu.VMEM((4,) + tile_count.shape, jnp.int32),
            pltpu.SMEM((4,) + tile_cols.shape, jnp.int32),
            pltpu.SMEM((4,) + tile_count.shape, jnp.int32),
            pltpu.VMEM((8,) + weights.shape[1:], bf),
            pltpu.VMEM((16, 128, WIDE * 128), bf),
            pltpu.VMEM((2, 6 * ROWS, width), bf),
            pltpu.VMEM((ROWS, width), bf),
            pltpu.VMEM((ROWS, width), bf),
            dma((5,)), dma((11,)), dma((11,)), dma((3,)), dma((3,)), dma((3,)), dma((3,)),
            dma((3,)), dma((3,)), dma((7,)), dma((8,)), dma, dma,
        ],
        compiler_params=pltpu.CompilerParams(collective_id=0, has_side_effects=True,
                                             vmem_limit_bytes=63 * 1024 * 1024),
        cost_estimate=pl.CostEstimate(flops=15_000_000_000, bytes_accessed=8_000_000, transcendentals=0),
        name="whole",
    )(betas, tiles, features, tile_cols, tile_count, weights)


def solution(mesh):
    in_specs = (
        P(None, "node", None),
        P(None, "node", None, None, None),
        P(None, "node", None),
        P(None, "node"),
        P("segment", None, None),
    )
    out_specs = P("segment", None, "node", None)
    small = mesh.shape["segment"] == 8 and mesh.shape["node"] == 4
    return jax.shard_map(
        whole_spans if small else on_device, mesh=mesh, in_specs=in_specs, out_specs=out_specs, check_vma=False
    )
```

```python
import jax
import jax.numpy as jnp
import numpy as np
from jax import lax
from jax.experimental import pallas as pl
from jax.experimental.pallas import tpu as pltpu
from jax.sharding import PartitionSpec as P


def with_halo(array, sides, width):
    for axis, dim in sides:
        count, length = (lax.axis_size(axis), array.shape[dim])
        up = [(i, (i + 1) % count) for i in range(count)]
        down = [(j, i) for i, j in up]
        last = lax.slice_in_dim(array, length - width, length, axis=dim)
        first = lax.slice_in_dim(array, 0, width, axis=dim)
        before = lax.ppermute(last, axis, up)
        after = lax.ppermute(first, axis, down)
        array = jnp.concatenate([before, array, after], axis=dim)
    return array


def passed_along(block, axis, distance):
    devices = range(lax.axis_size(axis))
    route = [(i - distance, i) for i in devices if i - distance in devices]
    return lax.ppermute(block, axis, route)


def layer_rows(window, masked, columns, initial, weight, beta_mix):
    tile_size = masked.shape[-1]
    feature_width = window.shape[-1]
    grouped = window.reshape(window.shape[0] // tile_size, tile_size, feature_width)
    picked = grouped[columns]
    aggregate = jnp.einsum("bkij,bkjd->bid", masked, picked, preferred_element_type=jnp.float32)
    aggregate = aggregate.reshape(-1, feature_width)
    support = (0.9 * aggregate + 0.1 * initial.astype(jnp.float32)).astype(jnp.bfloat16)
    branch = jnp.dot(support, weight, preferred_element_type=jnp.float32)
    combined = (1.0 - beta_mix) * support.astype(jnp.float32) + beta_mix * branch
    return jnp.maximum(combined, 0.0).astype(jnp.bfloat16)


def on_device(features, tiles, tile_cols, tile_count, weights):
    segments = lax.axis_size("segment")
    groups = lax.axis_size("node")
    segment_id = lax.axis_index("segment")
    group_id = lax.axis_index("node")
    spans = features.shape[0]
    per_group = tiles.shape[1]
    total_blocks = per_group * groups
    first_block = (group_id - 1) * per_group
    local_cols = (tile_cols - first_block + total_blocks) % total_blocks
    slot_ids = jnp.arange(tiles.shape[2], dtype=jnp.int32)
    live = (slot_ids[None, None, :] < tile_count[:, :, None]).astype(jnp.bfloat16)
    masked = tiles * live[:, :, :, None, None]
    beta_mix = jnp.log(0.5 / (segment_id.astype(jnp.float32) + 1.0) + 1.0)
    weight = weights[0]
    rows_here = features.shape[1]

    def step(step_no, state_pair):
        incoming, stored = state_pair
        offset_now = step_no - segment_id
        active = (offset_now >= 0) & (offset_now < spans)
        span_id = jnp.clip(offset_now, 0, spans - 1)
        initial = lax.dynamic_index_in_dim(features, span_id, 0, keepdims=False)
        layer_input = jnp.where(segment_id == 0, initial, incoming)
        window = with_halo(layer_input, (("node", 0),), rows_here)
        span_tiles = lax.dynamic_index_in_dim(masked, span_id, 0, keepdims=False)
        span_cols = lax.dynamic_index_in_dim(local_cols, span_id, 0, keepdims=False)
        result = layer_rows(window, span_tiles, span_cols, initial, weight, beta_mix)
        updated = lax.dynamic_update_index_in_dim(stored, result, span_id, 0)
        stored = jnp.where(active, updated, stored)
        incoming = passed_along(result, "segment", 1)
        return (incoming, stored)

    start_pair = (
        jnp.zeros(features.shape[1:], jnp.bfloat16),
        jnp.zeros(features.shape, jnp.bfloat16),
    )
    final_pair = lax.fori_loop(0, segments + spans - 1, step, start_pair)
    stored = final_pair[1]
    return stored[None]


MESH = pl.DeviceIdType.MESH
ROWS = 512
WIDE = 12


def whole_kernel(betas, tiles, feats, cols, counts, weight, out,
                 a_all, f_all, c_vm, n_vm, c_all, n_all, w_all, dense, hid, own_ref, send_ref,
                 loc, asem, arec, fsem, frec, csem, crec, nsem, nrec, wsem, wrec, osem, orec):
    seg = lax.axis_index("segment")
    g = lax.axis_index("node")
    c = seg % 2
    z = seg // 2
    span = z % 2
    xn = g + 1 - 2 * (g % 2)
    yn = (g + 2) % 4
    dn = 3 - g
    partner = (z + 1 - 2 * span) * 2 + c
    last = seg + 2 - 2 * span

    def at(start, size):
        return pl.ds(pl.multiple_of(start, size), size)

    def remote(src, dst, ssem, rsem, dev):
        return pltpu.make_async_remote_copy(src, dst, ssem, rsem, device_id=dev, device_id_type=MESH)

    barrier = pltpu.get_barrier_semaphore()
    for n in (xn, yn, dn):
        pl.semaphore_signal(barrier, inc=1, device_id={"node": n}, device_id_type=MESH)
    for d in range(1, 8):
        pl.semaphore_signal(barrier, inc=1, device_id={"segment": (seg + d) % 8}, device_id_type=MESH)
    pl.semaphore_wait(barrier, 10)

    local = [pltpu.make_async_copy(s, t, loc.at[k]) for k, (s, t) in enumerate((
        (cols, c_vm.at[g]), (counts, n_vm.at[g]), (feats.at[span], f_all.at[g]),
        (tiles.at[span], a_all.at[g]), (weight.at[0], w_all.at[seg])))]
    for cp in local:
        cp.start()

    small = []
    for d, n in enumerate((xn, yn, dn)):
        small.append(remote(cols, c_vm.at[g], csem.at[d], crec.at[d], {"node": n}))
        small.append(remote(counts, n_vm.at[g], nsem.at[d], nrec.at[d], {"node": n}))
    part = at(c * 256, 256)
    first = [remote(feats.at[span, part], f_all.at[g, part], fsem.at[d], frec.at[d], {"node": n})
             for d, n in enumerate((xn, yn, dn))]
    for cp in small + first:
        cp.start()

    low_copies = [remote(weight.at[0], w_all.at[seg], wsem.at[d], wrec.at[seg], {"segment": (seg + d + 1) % 8})
                  for d in range(7)]
    high_copies = [remote(weight.at[0], w_all.at[seg], wsem.at[d], wrec.at[seg], {"segment": 4 + (seg + d + 1) % 4})
                   for d in range(3)]

    @pl.when(z < 2)
    def _():
        for cp in low_copies:
            cp.start()

    front = pl.ds(2 * c, 2)
    inner = pl.ds(2 - c, 1)
    direct = [remote(tiles.at[span, rows], a_all.at[g, rows], asem.at[k], arec.at[k], {"node": n})
              for k, (rows, n) in enumerate(((front, xn), (front, yn), (inner, xn), (inner, yn)))]
    for cp in direct:
        cp.start()

    @pl.when(z >= 2)
    def _():
        for cp in high_copies:
            cp.start()

    for cp in local:
        cp.wait()
    for cp in small:
        cp.wait()
    meta = [pltpu.make_async_copy(c_vm, c_all, loc.at[0]), pltpu.make_async_copy(n_vm, n_all, loc.at[1])]
    for cp in meta:
        cp.start()
    for cp in meta:
        cp.wait()

    def densify(grp, from_row, count):
        def block(i, carry):
            row = from_row + i
            live = counts_of(grp, row)
            place = [(c_all[grp, span, row, k] - 4 * (grp - 1) + 16) % 16 for k in range(8)]
            place = [jnp.where(k < live, place[k], -1) for k in range(8)]

            def strip(r, carry):
                rows = at(r * 32, 32)
                part = [a_all[grp, row, k, rows, :].astype(jnp.float32) for k in range(8)]
                for j in range(WIDE):
                    total = None
                    for k in range(8):
                        term = part[k] * jnp.where(place[k] == j, 1.0, 0.0)
                        total = term if total is None else total + term
                    dense[grp * 4 + row, rows, j * 128:(j + 1) * 128] = total.astype(jnp.bfloat16)
                return carry

            return lax.fori_loop(0, 4, strip, carry)

        lax.fori_loop(0, count, block, 0)

    def counts_of(grp, row):
        return n_all[grp, span, row]

    densify(g, 0, 4)

    via = xn * (1 - c) + yn * c
    beyond = yn * (1 - c) + xn * c
    peer = seg + 1 - 2 * c

    def across_chip(piece, k):
        return remote(piece, piece, asem.at[k], arec.at[k], {"segment": peer})

    for cp in first:
        cp.wait_recv()
    first_share = [across_chip(f_all.at[n, part], 10 + d) for d, n in enumerate((xn, yn, dn))]
    for cp in first_share:
        cp.start()
    for k in (c, 1 - c):
        remote(tiles.at[span, front], a_all.at[g, front], asem.at[k], arec.at[k], {"node": xn}).wait_recv()
        if k is c:
            onward = [remote(a_all.at[via, 2 * c + i], a_all.at[via, 2 * c + i], asem.at[4 + i], arec.at[4 + i],
                             {"node": beyond}) for i in range(2)]
            for cp in onward:
                cp.start()
    edge = [across_chip(a_all.at[n, 3 * c], 8 + k) for k, n in enumerate((xn, yn))]
    for cp in edge:
        cp.start()
    densify(xn, 2 * c, 2)
    densify(yn, 2 * c, 2)

    def put(buf, grp, value):
        hid[buf, at((grp + 1) * ROWS, ROWS), :] = value

        @pl.when(grp == 3)
        def _():
            hid[buf, 0:ROWS, :] = value

        @pl.when(grp == 0)
        def _():
            hid[buf, 5 * ROWS:6 * ROWS, :] = value

    for cp in first_share:
        cp.wait_recv()

    def start(grp, carry):
        put(0, grp, f_all[grp])
        return carry

    lax.fori_loop(0, 4, start, 0)
    direct[2].wait_recv()
    densify(xn, 2 - c, 1)
    direct[3].wait_recv()
    densify(yn, 2 - c, 1)
    edge[0].wait_recv()
    densify(xn, 3 - 3 * c, 1)
    edge[1].wait_recv()
    densify(yn, 3 - 3 * c, 1)
    shares = []
    for i in range(2):
        onward[i].wait_recv()
        p = a_all.at[dn, 2 * c + i]
        shares.append(remote(p, p, asem.at[6 + i], arec.at[6 + i], {"segment": peer}))
        shares[i].start()

    def weight_here(l):
        @pl.when(l != seg)
        def _():
            remote(weight.at[0], w_all.at[l], wsem.at[0], wrec.at[l], {"segment": peer}).wait_recv()

    def group_rows(l, grp, window):
        lhs = dense[pl.ds(grp * 4, 4)].reshape(ROWS, WIDE * 128)
        agg = jnp.dot(lhs, window, preferred_element_type=jnp.float32)
        sup = (0.9 * agg + 0.1 * f_all[grp].astype(jnp.float32)).astype(jnp.bfloat16)
        branch = jnp.dot(sup, w_all[l], preferred_element_type=jnp.float32)
        beta = betas[l]
        res = (1.0 - beta) * sup.astype(jnp.float32) + beta * branch
        return jnp.maximum(res, 0.0).astype(jnp.bfloat16)

    def window_of(buf, grp):
        return hid[buf, pl.ds(pl.multiple_of(grp * ROWS, ROWS), 3 * ROWS), :]

    def layer(l, carry):
        cur = l % 2
        weight_here(l)

        def one(grp, carry):
            put(1 - cur, grp, group_rows(l, grp, window_of(cur, grp)))
            return carry

        return lax.fori_loop(0, 4, one, carry)

    weight_here(0)

    def early(i, carry):
        grp = (dn + 1 + i) % 4
        put(1, grp, group_rows(0, grp, window_of(0, grp)))
        return carry

    lax.fori_loop(0, 3, early, 0)
    densify(dn, 2 * c, 2)
    for cp in shares:
        cp.wait_recv()
    densify(dn, 2 - 2 * c, 2)
    put(1, dn, group_rows(0, dn, window_of(0, dn)))
    lax.fori_loop(1, last - 1, layer, 0)
    cur = (last - 1) % 2
    low_at = at((g + 1) * ROWS, ROWS)
    across = remote(send_ref, out.at[0, span], osem, orec, {"segment": partner})

    @pl.when(span == 1)
    def _():
        send_ref[...] = hid[cur, low_at, :]
        across.start()

    @pl.when(span == 0)
    def _():
        own_ref[...] = hid[cur, low_at, :]

    weight_here(last - 1)

    def near(i, carry):
        grp = (g + 3 + i) % 4
        hid[1 - cur, at(i * ROWS, ROWS), :] = group_rows(last - 1, grp, window_of(cur, grp))
        return carry

    lax.fori_loop(0, 3, near, 0)
    weight_here(last)
    high = group_rows(last, g, hid[1 - cur, 0:3 * ROWS, :])

    @pl.when(span == 0)
    def _():
        send_ref[...] = high
        across.start()

    @pl.when(span == 1)
    def _():
        own_ref[...] = high

    mine = pltpu.make_async_copy(own_ref, out.at[0, span], loc.at[0])
    mine.start()

    def rest(l, carry):
        weight_here(l)
        return carry

    lax.fori_loop(last + 1, jnp.where(z < 2, 4, 8), rest, 0)
    for cp in direct + onward + shares + edge + first + first_share:
        cp.wait_send()

    @pl.when(z < 2)
    def _():
        for cp in low_copies:
            cp.wait_send()

    @pl.when(z >= 2)
    def _():
        for cp in high_copies:
            cp.wait_send()

    mine.wait()
    across.wait()


def whole_spans(features, tiles, tile_cols, tile_count, weights):
    hbm = pl.BlockSpec(memory_space=pltpu.HBM)
    bf = jnp.bfloat16
    dma = pltpu.SemaphoreType.DMA
    betas = jnp.asarray(np.log(0.5 / (np.arange(8, dtype=np.float32) + 1.0) + 1.0), jnp.float32)
    width = features.shape[-1]
    return pl.pallas_call(
        whole_kernel,
        out_shape=jax.ShapeDtypeStruct((1,) + features.shape, bf),
        in_specs=[pl.BlockSpec(memory_space=pltpu.SMEM)] + [hbm] * 5,
        out_specs=hbm,
        scratch_shapes=[
            pltpu.VMEM((4,) + tiles.shape[1:], bf),
            pltpu.VMEM((4,) + features.shape[1:], bf),
            pltpu.VMEM((4,) + tile_cols.shape, jnp.int32),
            pltpu.VMEM((4,) + tile_count.shape, jnp.int32),
            pltpu.SMEM((4,) + tile_cols.shape, jnp.int32),
            pltpu.SMEM((4,) + tile_count.shape, jnp.int32),
            pltpu.VMEM((8,) + weights.shape[1:], bf),
            pltpu.VMEM((16, 128, WIDE * 128), bf),
            pltpu.VMEM((2, 6 * ROWS, width), bf),
            pltpu.VMEM((ROWS, width), bf),
            pltpu.VMEM((ROWS, width), bf),
            dma((5,)), dma((13,)), dma((13,)), dma((3,)), dma((3,)), dma((3,)), dma((3,)),
            dma((3,)), dma((3,)), dma((7,)), dma((8,)), dma, dma,
        ],
        compiler_params=pltpu.CompilerParams(collective_id=0, has_side_effects=True,
                                             vmem_limit_bytes=63 * 1024 * 1024),
        cost_estimate=pl.CostEstimate(flops=15_000_000_000, bytes_accessed=8_000_000, transcendentals=0),
        name="whole",
    )(betas, tiles, features, tile_cols, tile_count, weights)


def solution(mesh):
    in_specs = (
        P(None, "node", None),
        P(None, "node", None, None, None),
        P(None, "node", None),
        P(None, "node"),
        P("segment", None, None),
    )
    out_specs = P("segment", None, "node", None)
    small = mesh.shape["segment"] == 8 and mesh.shape["node"] == 4
    return jax.shard_map(
        whole_spans if small else on_device, mesh=mesh, in_specs=in_specs, out_specs=out_specs, check_vma=False
    )
```

```python
import jax
import jax.numpy as jnp
import numpy as np
from jax import lax
from jax.experimental import pallas as pl
from jax.experimental.pallas import tpu as pltpu
from jax.sharding import PartitionSpec as P


def with_halo(array, sides, width):
    for axis, dim in sides:
        count, length = (lax.axis_size(axis), array.shape[dim])
        up = [(i, (i + 1) % count) for i in range(count)]
        down = [(j, i) for i, j in up]
        last = lax.slice_in_dim(array, length - width, length, axis=dim)
        first = lax.slice_in_dim(array, 0, width, axis=dim)
        before = lax.ppermute(last, axis, up)
        after = lax.ppermute(first, axis, down)
        array = jnp.concatenate([before, array, after], axis=dim)
    return array


def passed_along(block, axis, distance):
    devices = range(lax.axis_size(axis))
    route = [(i - distance, i) for i in devices if i - distance in devices]
    return lax.ppermute(block, axis, route)


def layer_rows(window, masked, columns, initial, weight, beta_mix):
    tile_size = masked.shape[-1]
    feature_width = window.shape[-1]
    grouped = window.reshape(window.shape[0] // tile_size, tile_size, feature_width)
    picked = grouped[columns]
    aggregate = jnp.einsum("bkij,bkjd->bid", masked, picked, preferred_element_type=jnp.float32)
    aggregate = aggregate.reshape(-1, feature_width)
    support = (0.9 * aggregate + 0.1 * initial.astype(jnp.float32)).astype(jnp.bfloat16)
    branch = jnp.dot(support, weight, preferred_element_type=jnp.float32)
    combined = (1.0 - beta_mix) * support.astype(jnp.float32) + beta_mix * branch
    return jnp.maximum(combined, 0.0).astype(jnp.bfloat16)


def on_device(features, tiles, tile_cols, tile_count, weights):
    segments = lax.axis_size("segment")
    groups = lax.axis_size("node")
    segment_id = lax.axis_index("segment")
    group_id = lax.axis_index("node")
    spans = features.shape[0]
    per_group = tiles.shape[1]
    total_blocks = per_group * groups
    first_block = (group_id - 1) * per_group
    local_cols = (tile_cols - first_block + total_blocks) % total_blocks
    slot_ids = jnp.arange(tiles.shape[2], dtype=jnp.int32)
    live = (slot_ids[None, None, :] < tile_count[:, :, None]).astype(jnp.bfloat16)
    masked = tiles * live[:, :, :, None, None]
    beta_mix = jnp.log(0.5 / (segment_id.astype(jnp.float32) + 1.0) + 1.0)
    weight = weights[0]
    rows_here = features.shape[1]

    def step(step_no, state_pair):
        incoming, stored = state_pair
        offset_now = step_no - segment_id
        active = (offset_now >= 0) & (offset_now < spans)
        span_id = jnp.clip(offset_now, 0, spans - 1)
        initial = lax.dynamic_index_in_dim(features, span_id, 0, keepdims=False)
        layer_input = jnp.where(segment_id == 0, initial, incoming)
        window = with_halo(layer_input, (("node", 0),), rows_here)
        span_tiles = lax.dynamic_index_in_dim(masked, span_id, 0, keepdims=False)
        span_cols = lax.dynamic_index_in_dim(local_cols, span_id, 0, keepdims=False)
        result = layer_rows(window, span_tiles, span_cols, initial, weight, beta_mix)
        updated = lax.dynamic_update_index_in_dim(stored, result, span_id, 0)
        stored = jnp.where(active, updated, stored)
        incoming = passed_along(result, "segment", 1)
        return (incoming, stored)

    start_pair = (
        jnp.zeros(features.shape[1:], jnp.bfloat16),
        jnp.zeros(features.shape, jnp.bfloat16),
    )
    final_pair = lax.fori_loop(0, segments + spans - 1, step, start_pair)
    stored = final_pair[1]
    return stored[None]


MESH = pl.DeviceIdType.MESH
ROWS = 512
WIDE = 12


def whole_kernel(betas, tiles, feats, cols, counts, weight, out,
                 a_all, f_all, c_vm, n_vm, c_all, n_all, w_all, dense, hid, own_ref, send_ref,
                 loc, asem, arec, fsem, frec, csem, crec, nsem, nrec, wsem, wrec, osem, orec):
    seg = lax.axis_index("segment")
    g = lax.axis_index("node")
    c = seg % 2
    z = seg // 2
    span = z % 2
    xn = g + 1 - 2 * (g % 2)
    yn = (g + 2) % 4
    dn = 3 - g
    partner = (z + 1 - 2 * span) * 2 + c
    last = seg + 2 - 2 * span

    def at(start, size):
        return pl.ds(pl.multiple_of(start, size), size)

    def remote(src, dst, ssem, rsem, dev):
        return pltpu.make_async_remote_copy(src, dst, ssem, rsem, device_id=dev, device_id_type=MESH)

    barrier = pltpu.get_barrier_semaphore()
    for n in (xn, yn, dn):
        pl.semaphore_signal(barrier, inc=1, device_id={"node": n}, device_id_type=MESH)
    for d in range(1, 8):
        pl.semaphore_signal(barrier, inc=1, device_id={"segment": (seg + d) % 8}, device_id_type=MESH)
    pl.semaphore_wait(barrier, 10)

    local = [pltpu.make_async_copy(s, t, loc.at[k]) for k, (s, t) in enumerate((
        (cols, c_vm.at[g]), (counts, n_vm.at[g]), (feats.at[span], f_all.at[g]),
        (tiles.at[span], a_all.at[g]), (weight.at[0], w_all.at[seg])))]
    for cp in local:
        cp.start()

    small = []
    for d, n in enumerate((xn, yn, dn)):
        small.append(remote(cols, c_vm.at[g], csem.at[d], crec.at[d], {"node": n}))
        small.append(remote(counts, n_vm.at[g], nsem.at[d], nrec.at[d], {"node": n}))
    part = at(c * 256, 256)
    first = [remote(feats.at[span, part], f_all.at[g, part], fsem.at[d], frec.at[d], {"node": n})
             for d, n in enumerate((xn, yn, dn))]
    for cp in small + first:
        cp.start()

    low_copies = [remote(weight.at[0], w_all.at[seg], wsem.at[d], wrec.at[seg], {"segment": (seg + d + 1) % 8})
                  for d in range(7)]
    high_copies = [remote(weight.at[0], w_all.at[seg], wsem.at[d], wrec.at[seg], {"segment": 4 + (seg + d + 1) % 4})
                   for d in range(3)]

    @pl.when(z < 2)
    def _():
        for cp in low_copies:
            cp.start()

    front = pl.ds(2 * c, 2)
    inner = pl.ds(2 - c, 1)
    direct = [remote(tiles.at[span, rows], a_all.at[g, rows], asem.at[k], arec.at[k], {"node": n})
              for k, (rows, n) in enumerate(((front, xn), (front, yn), (inner, xn), (inner, yn)))]
    for cp in direct[:2]:
        cp.start()

    @pl.when(z >= 2)
    def _():
        for cp in high_copies:
            cp.start()

    for cp in local:
        cp.wait()
    for cp in small:
        cp.wait()
    meta = [pltpu.make_async_copy(c_vm, c_all, loc.at[0]), pltpu.make_async_copy(n_vm, n_all, loc.at[1])]
    for cp in meta:
        cp.start()
    for cp in meta:
        cp.wait()

    def densify(grp, from_row, count):
        def block(i, carry):
            row = from_row + i
            live = counts_of(grp, row)
            place = [(c_all[grp, span, row, k] - 4 * (grp - 1) + 16) % 16 for k in range(8)]
            place = [jnp.where(k < live, place[k], -1) for k in range(8)]

            def strip(r, carry):
                rows = at(r * 32, 32)
                part = [a_all[grp, row, k, rows, :].astype(jnp.float32) for k in range(8)]
                for j in range(WIDE):
                    total = None
                    for k in range(8):
                        term = part[k] * jnp.where(place[k] == j, 1.0, 0.0)
                        total = term if total is None else total + term
                    dense[grp * 4 + row, rows, j * 128:(j + 1) * 128] = total.astype(jnp.bfloat16)
                return carry

            return lax.fori_loop(0, 4, strip, carry)

        lax.fori_loop(0, count, block, 0)

    def counts_of(grp, row):
        return n_all[grp, span, row]

    densify(g, 0, 4)

    via = xn * (1 - c) + yn * c
    beyond = yn * (1 - c) + xn * c
    peer = seg + 1 - 2 * c

    def across_chip(piece, k):
        return remote(piece, piece, asem.at[k], arec.at[k], {"segment": peer})

    for cp in first:
        cp.wait_recv()
    first_share = [across_chip(f_all.at[n, part], 10 + d) for d, n in enumerate((xn, yn, dn))]
    for cp in first_share:
        cp.start()
    for k in (c, 1 - c):
        remote(tiles.at[span, front], a_all.at[g, front], asem.at[k], arec.at[k], {"node": xn}).wait_recv()
        if k is c:
            onward = [remote(a_all.at[via, 2 * c + i], a_all.at[via, 2 * c + i], asem.at[4 + i], arec.at[4 + i],
                             {"node": beyond}) for i in range(2)]
            for cp in onward:
                cp.start()
    edge = [across_chip(a_all.at[n, 3 * c], 8 + k) for k, n in enumerate((xn, yn))]
    for cp in direct[2:] + edge:
        cp.start()
    densify(xn, 2 * c, 2)
    densify(yn, 2 * c, 2)

    def put(buf, grp, value):
        hid[buf, at((grp + 1) * ROWS, ROWS), :] = value

        @pl.when(grp == 3)
        def _():
            hid[buf, 0:ROWS, :] = value

        @pl.when(grp == 0)
        def _():
            hid[buf, 5 * ROWS:6 * ROWS, :] = value

    for cp in first_share:
        cp.wait_recv()

    def start(grp, carry):
        put(0, grp, f_all[grp])
        return carry

    lax.fori_loop(0, 4, start, 0)
    shares = []
    for i in range(2):
        onward[i].wait_recv()
        p = a_all.at[dn, 2 * c + i]
        shares.append(remote(p, p, asem.at[6 + i], arec.at[6 + i], {"segment": peer}))
        shares[i].start()

    direct[2].wait_recv()
    densify(xn, 2 - c, 1)
    direct[3].wait_recv()
    densify(yn, 2 - c, 1)
    edge[0].wait_recv()
    densify(xn, 3 - 3 * c, 1)
    edge[1].wait_recv()
    densify(yn, 3 - 3 * c, 1)
    def weight_here(l):
        @pl.when(l != seg)
        def _():
            remote(weight.at[0], w_all.at[l], wsem.at[0], wrec.at[l], {"segment": peer}).wait_recv()

    def group_rows(l, grp, window):
        lhs = dense[pl.ds(grp * 4, 4)].reshape(ROWS, WIDE * 128)
        agg = jnp.dot(lhs, window, preferred_element_type=jnp.float32)
        sup = (0.9 * agg + 0.1 * f_all[grp].astype(jnp.float32)).astype(jnp.bfloat16)
        branch = jnp.dot(sup, w_all[l], preferred_element_type=jnp.float32)
        beta = betas[l]
        res = (1.0 - beta) * sup.astype(jnp.float32) + beta * branch
        return jnp.maximum(res, 0.0).astype(jnp.bfloat16)

    def window_of(buf, grp):
        return hid[buf, pl.ds(pl.multiple_of(grp * ROWS, ROWS), 3 * ROWS), :]

    def layer(l, carry):
        cur = l % 2
        weight_here(l)

        def one(grp, carry):
            put(1 - cur, grp, group_rows(l, grp, window_of(cur, grp)))
            return carry

        return lax.fori_loop(0, 4, one, carry)

    weight_here(0)

    def early(i, carry):
        grp = (dn + 1 + i) % 4
        put(1, grp, group_rows(0, grp, window_of(0, grp)))
        return carry

    lax.fori_loop(0, 3, early, 0)
    densify(dn, 2 * c, 2)
    for cp in shares:
        cp.wait_recv()
    densify(dn, 2 - 2 * c, 2)
    put(1, dn, group_rows(0, dn, window_of(0, dn)))
    lax.fori_loop(1, last - 1, layer, 0)
    cur = (last - 1) % 2
    low_at = at((g + 1) * ROWS, ROWS)
    across = remote(send_ref, out.at[0, span], osem, orec, {"segment": partner})

    @pl.when(span == 1)
    def _():
        send_ref[...] = hid[cur, low_at, :]
        across.start()

    @pl.when(span == 0)
    def _():
        own_ref[...] = hid[cur, low_at, :]

    weight_here(last - 1)

    def near(i, carry):
        grp = (g + 3 + i) % 4
        hid[1 - cur, at(i * ROWS, ROWS), :] = group_rows(last - 1, grp, window_of(cur, grp))
        return carry

    lax.fori_loop(0, 3, near, 0)
    weight_here(last)
    high = group_rows(last, g, hid[1 - cur, 0:3 * ROWS, :])

    @pl.when(span == 0)
    def _():
        send_ref[...] = high
        across.start()

    @pl.when(span == 1)
    def _():
        own_ref[...] = high

    mine = pltpu.make_async_copy(own_ref, out.at[0, span], loc.at[0])
    mine.start()

    def rest(l, carry):
        weight_here(l)
        return carry

    lax.fori_loop(last + 1, jnp.where(z < 2, 4, 8), rest, 0)
    for cp in direct + onward + shares + edge + first + first_share:
        cp.wait_send()

    @pl.when(z < 2)
    def _():
        for cp in low_copies:
            cp.wait_send()

    @pl.when(z >= 2)
    def _():
        for cp in high_copies:
            cp.wait_send()

    mine.wait()
    across.wait()


def whole_spans(features, tiles, tile_cols, tile_count, weights):
    hbm = pl.BlockSpec(memory_space=pltpu.HBM)
    bf = jnp.bfloat16
    dma = pltpu.SemaphoreType.DMA
    betas = jnp.asarray(np.log(0.5 / (np.arange(8, dtype=np.float32) + 1.0) + 1.0), jnp.float32)
    width = features.shape[-1]
    return pl.pallas_call(
        whole_kernel,
        out_shape=jax.ShapeDtypeStruct((1,) + features.shape, bf),
        in_specs=[pl.BlockSpec(memory_space=pltpu.SMEM)] + [hbm] * 5,
        out_specs=hbm,
        scratch_shapes=[
            pltpu.VMEM((4,) + tiles.shape[1:], bf),
            pltpu.VMEM((4,) + features.shape[1:], bf),
            pltpu.VMEM((4,) + tile_cols.shape, jnp.int32),
            pltpu.VMEM((4,) + tile_count.shape, jnp.int32),
            pltpu.SMEM((4,) + tile_cols.shape, jnp.int32),
            pltpu.SMEM((4,) + tile_count.shape, jnp.int32),
            pltpu.VMEM((8,) + weights.shape[1:], bf),
            pltpu.VMEM((16, 128, WIDE * 128), bf),
            pltpu.VMEM((2, 6 * ROWS, width), bf),
            pltpu.VMEM((ROWS, width), bf),
            pltpu.VMEM((ROWS, width), bf),
            dma((5,)), dma((13,)), dma((13,)), dma((3,)), dma((3,)), dma((3,)), dma((3,)),
            dma((3,)), dma((3,)), dma((7,)), dma((8,)), dma, dma,
        ],
        compiler_params=pltpu.CompilerParams(collective_id=0, has_side_effects=True,
                                             vmem_limit_bytes=63 * 1024 * 1024),
        cost_estimate=pl.CostEstimate(flops=15_000_000_000, bytes_accessed=8_000_000, transcendentals=0),
        name="whole",
    )(betas, tiles, features, tile_cols, tile_count, weights)


def solution(mesh):
    in_specs = (
        P(None, "node", None),
        P(None, "node", None, None, None),
        P(None, "node", None),
        P(None, "node"),
        P("segment", None, None),
    )
    out_specs = P("segment", None, "node", None)
    small = mesh.shape["segment"] == 8 and mesh.shape["node"] == 4
    return jax.shard_map(
        whole_spans if small else on_device, mesh=mesh, in_specs=in_specs, out_specs=out_specs, check_vma=False
    )
```
